256 devices in a mesh: leaf: 64 (over z, x, core), vec: 4 (over y).
Axes of the slice: x: 4, y: 4, z: 8, core: 2. Of those that a mesh axis runs over, the one named last changes fastest.
Arguments:
- vectors: bfloat16 [64, 524288], P('vec', 'leaf'), may hold values from -6 to 6
- points: float32 [3, 524288], P(None, ('leaf', 'vec')), may hold values from 0 to 1
- leaf_basis: bfloat16 [4096, 64, 128], P('leaf'), may hold values from -0.5 to 0.5
- local_transfer: bfloat16 [8192, 64, 64], P('leaf'), may hold values from -0.625 to 0.625
- local_coupling: bfloat16 [8192, 64, 64], P('leaf'), may hold values from -0.75 to 0.75
- upper_transfer: bfloat16 [64, 64, 64], replicated, may hold values from -0.625 to 0.625
- upper_coupling: bfloat16 [64, 64, 64], replicated, may hold values from -0.75 to 0.75
- far_anchor: int32 [16384, 1], P('leaf'), may hold values from 0 to 63; in each aligned block of 256 rows (0 to 255, 256 to 511, ...) at most 8 rows name the same one
- far_leaves: int32 [16384, 2], P('leaf'), may hold values from 0 to 63
- far_block: bfloat16 [16384, 64, 64], P('leaf'), may hold values from -0.5 to 0.5
- near_cols: int32 [4096, 8], P('leaf'), may hold values from 0 to 4095, as said below
Outputs:
- product: float32 [64, 524288], P('vec', 'leaf')
The draws below stay inside these ranges and needn't reach their ends.
Inputs may be any that keep to these rules, and one draw needn't show every extreme that they name: near_cols[t, 0] = t, and every entry lies within 8 leaves of t. `far_anchor`: among the 256 rows of one index of leaf, no value is named more than 8 times, and in every draw some value is named exactly 8 times.
All inputs are finite; a program needn't handle non-finite values.
Results may differ from the reference program's by a relative error of at most 0.0075.
Values may be sent and summed in bfloat16 or wider, within the bound.
No kernel may reach another device: no remote copies, remote signals or barrier semaphores. Data moves between devices by JAX's collectives and lax.ppermute only.
A program may use at most 128 MiB of HBM per device.

```python
import math
import jax
import jax.numpy as jnp
import numpy as np
from jax import lax

LEAF = 128
RANK = 64
NV = 64
NEAR = 8
REACH = 8
LEAF_DEV = 64
PAIRS_DEV = 256
LEAVES = 4096
POINTS = 524288
PAIRS = 16384
CAP = 8
N_LEAF = 64


def draw_near_cols(key, part):
    key = jax.random.fold_in(key, 11)
    leaf_ids = jnp.arange(LEAVES, dtype=jnp.int32)[:, None]
    offsets = jax.random.randint(key, (LEAVES, NEAR), -REACH, REACH + 1, dtype=jnp.int32)
    offsets = offsets.at[:, 0].set(0)
    return jnp.clip(leaf_ids + offsets, 0, LEAVES - 1).astype(jnp.int32)


def plant(result, stream_key, low, largest):
    spot = [jax.random.randint(jax.random.fold_in(stream_key, axis), (), 0, length) for axis, length in enumerate(result.shape)]
    longest = result.shape.index(max(result.shape))
    beside = spot[:longest] + [(spot[longest] + 1) % result.shape[longest]] + spot[longest + 1:]
    return result.at[tuple(spot)].set(low).at[tuple(beside)].set(largest)


def steps_of(rng, shape, pieces, low, high):
    factor_of = 1.0
    for dim, blocks in pieces:
        draws = jax.random.uniform(jax.random.fold_in(jax.random.fold_in(rng, 6), dim), (blocks,), jnp.float32, low / len(pieces), high / len(pieces))
        factor_of = factor_of * jnp.repeat(jnp.exp(draws), shape[dim] // blocks).reshape((-1,) + (1,) * (len(shape) - 1 - dim))
    return factor_of


def routed_block(stream_key, own, number, rows, count, top, most, skew):
    order = jax.random.permutation(stream_key, count)
    packed, common = load_shares(count, rows * top, most, skew, True), load_shares(count, rows * top, most, skew, False)
    places = jnp.arange(count)

    def named(sizes, rotation):
        used = int((sizes > 0).sum())
        fixed = max(1, used // 4)
        moved = fixed + (places - fixed + rotation * (used - fixed)) % max(1, count - fixed)
        return jnp.zeros((count,), jnp.int32).at[order[jnp.where(places < fixed, places, moved)]].set(jnp.asarray(sizes, jnp.int32))

    sizes = jnp.where(number % 4 == 0, named(packed, number // 4), named(common, number - number // 4 - 1))
    mixed = jax.random.permutation(jax.random.fold_in(own, 3), count)
    donor, receiver = mixed[0:count // 2 * 2:2], mixed[1:count // 2 * 2:2]
    margin = jnp.minimum(sizes[donor] - 1, most - sizes[receiver]) // 2
    margin = jnp.where((donor == order[0]) | (receiver == order[0]) | (sizes[receiver] == 0), 0, jnp.maximum(margin, 0))
    moved = jax.random.randint(jax.random.fold_in(own, 4), (count // 2,), 0, 1 << 20) % (margin + 1)
    sizes = sizes.at[donor].add(-moved).at[receiver].add(moved)
    labels = jnp.searchsorted(jnp.cumsum(sizes), jnp.arange(rows * top), side="right").astype(jnp.int32)
    table = labels.reshape(top, rows).T
    table = table[jax.random.permutation(jax.random.fold_in(own, 1), rows)]
    rotation = jax.random.randint(jax.random.fold_in(own, 2), (rows, 1), 0, top)
    return jnp.take_along_axis(table, (jnp.arange(top)[None, :] + rotation) % top, axis=1)


def load_shares(number_of, total, bound, slope, full):
    weights = [(1 << 20) // math.isqrt(rank ** slope) + 1 for rank in range(1, number_of + 1)]
    largest = bound if full else min(bound, max(-(-total // number_of), total * weights[0] // sum(weights)))
    least = 1 if total - largest >= number_of - 1 else 0
    given, surplus = [largest] + [least] * (number_of - 1), total - largest - least * (number_of - 1)
    while surplus > 0:
        movable = [i for i in range(1, number_of) if given[i] < largest] or [i for i in range(1, number_of) if given[i] < bound]
        whole, left = sum([weights[i] for i in movable]), surplus
        for i in movable:
            more = min(bound - given[i], max(1, left * weights[i] // whole), surplus)
            given[i] = given[i] + more
            surplus = surplus - more
    return np.array(given)


def normal_values(key, shape, deviation, most, split=(), kind=jnp.bfloat16):
    result = jax.random.normal(key, shape, jnp.float32) * deviation
    if len(split) > 0:
        result = steps_of(key, shape, split, -0.22, 0.18) * result
    return jnp.clip(result, min=-most, max=most).astype(kind)


def setup_inputs(seed: int = 0) -> dict:
    key_list = jax.random.split(jax.random.key(seed), 12)
    vectors = normal_values(key_list[0], (NV, POINTS), 1.0, 6.0, ((0, 4), (1, 64)))
    points = jnp.clip(1.0 * jax.random.uniform(key_list[1], (3, POINTS), jnp.float32) ** steps_of(key_list[1], (3, POINTS), ((1, 256),), -0.2, 0.2), 0.0, 1.0)
    leaf_basis = normal_values(key_list[2], (LEAVES, RANK, LEAF), LEAF ** -0.5, 0.5, ((0, 64),))
    local_transfer = normal_values(key_list[3], (2 * LEAVES, RANK, RANK), (3 * RANK // 2) ** -0.5, 0.625, ((0, 64),))
    local_coupling = normal_values(key_list[4], (2 * LEAVES, RANK, RANK), RANK ** -0.5, 0.75, ((0, 64),))
    upper_transfer = normal_values(key_list[5], (N_LEAF, RANK, RANK), (3 * RANK // 2) ** -0.5, 0.625)
    upper_coupling = normal_values(key_list[6], (N_LEAF, RANK, RANK), RANK ** -0.5, 0.75)
    far_anchor_keys = jax.random.split(jax.random.fold_in(key_list[7], 1), PAIRS // PAIRS_DEV)
    far_anchor_turns = jax.random.permutation(jax.random.fold_in(key_list[7], 3), PAIRS // PAIRS_DEV)
    far_anchor = jax.vmap(lambda own, number: routed_block(jax.random.fold_in(key_list[7], 2), own, number, PAIRS_DEV, N_LEAF, 1, CAP, 2))(far_anchor_keys, far_anchor_turns).reshape((PAIRS, 1))
    far_leaves = plant(jax.random.randint(key_list[8], (PAIRS, 2), 0, LEAF_DEV), jax.random.fold_in(key_list[8], 1), 0, LEAF_DEV - 1).astype(jnp.int32)
    far_block = normal_values(key_list[9], (PAIRS, RANK, RANK), (2 * RANK) ** -0.5, 0.5, ((0, 64),))
    near_cols = draw_near_cols(jax.random.fold_in(key_list[11], 71), 0)
    return {"vectors": vectors, "points": points, "leaf_basis": leaf_basis, "local_transfer": local_transfer, "local_coupling": local_coupling, "upper_transfer": upper_transfer, "upper_coupling": upper_coupling, "far_anchor": far_anchor, "far_leaves": far_leaves, "far_block": far_block, "near_cols": near_cols}


kernel_scale = 1.0 / 64.0
delta_sq = 0.0025

def reference(vectors, points, leaf_basis, local_transfer, local_coupling, upper_transfer, upper_coupling, far_anchor, far_leaves, far_block, near_cols):
    highest = lax.Precision.HIGHEST
    top_depth = N_LEAF.bit_length() - 1
    local_depth = LEAF_DEV.bit_length() - 1
    total_depth = top_depth + local_depth
    x_leaf = vectors.reshape(NV, LEAVES, LEAF)
    coeff = jnp.einsum('vtp,tkp->tvk', x_leaf.astype(jnp.float32), leaf_basis.astype(jnp.float32), precision=highest)
    transfer = local_transfer.astype(jnp.float32).reshape(N_LEAF, 2 * LEAF_DEV, RANK, RANK)
    coupling = local_coupling.astype(jnp.float32).reshape(N_LEAF, 2 * LEAF_DEV, RANK, RANK)
    upper_t = upper_transfer.astype(jnp.float32)
    upper_c = upper_coupling.astype(jnp.float32)

    def matrices(tree_depth):
        if tree_depth >= top_depth:
            start = 2 ** (tree_depth - top_depth)
            return (transfer[:, start:2 * start].reshape(-1, RANK, RANK), coupling[:, start:2 * start].reshape(-1, RANK, RANK))
        start = 2 ** tree_depth
        return (upper_t[start:2 * start], upper_c[start:2 * start])
    levels = {total_depth: coeff}
    current = coeff
    for tree_depth in range(total_depth, 1, -1):
        move_mat, _ = matrices(tree_depth)
        product = jnp.einsum('nvk,nkl->nvl', current, move_mat, precision=highest)
        current = product.reshape(-1, 2, NV, RANK).sum(1)
        levels[tree_depth - 1] = current
    downward = None
    for tree_depth in range(1, total_depth + 1):
        move_mat, pair_mat = matrices(tree_depth)
        coeffs = levels[tree_depth]
        node_count = coeffs.shape[0]
        sibling = coeffs.reshape(node_count // 2, 2, NV, RANK)[:, ::-1].reshape(node_count, NV, RANK)
        coupled = jnp.einsum('nvk,nkl->nvl', sibling, pair_mat, precision=highest)
        if downward is None:
            downward = coupled
        else:
            parent = jnp.repeat(downward, 2, axis=0)
            downward = jnp.einsum('nvl,nkl->nvk', parent, move_mat, precision=highest) + coupled
    pair_owner = jnp.arange(PAIRS, dtype=jnp.int32) // PAIRS_DEV
    source = (far_anchor[:, 0] * LEAF_DEV + far_leaves[:, 0]).astype(jnp.int32)
    target = (pair_owner * LEAF_DEV + far_leaves[:, 1]).astype(jnp.int32)
    sent = coeff.astype(jnp.bfloat16)
    fetched = jnp.take(sent, source, axis=0).astype(jnp.float32)
    contrib = jnp.einsum('pvk,pkl->pvl', fetched, far_block.astype(jnp.float32), precision=highest)
    far_sum = jax.ops.segment_sum(contrib, target, num_segments=LEAVES)
    leaf_local = (downward + far_sum).astype(jnp.bfloat16)
    far_part = jnp.einsum('tvk,tkp->vtp', leaf_local.astype(jnp.float32), leaf_basis.astype(jnp.float32), precision=highest)
    coords = points.reshape(3, LEAVES, LEAF)
    group_size = min(8, LEAVES)
    groups = LEAVES // group_size

    def near_group(inputs):
        col_ids, targets = inputs
        source_pts = jnp.take(coords, col_ids, axis=1)
        delta_x = targets[0][:, None, :, None] - source_pts[0][:, :, None, :]
        delta_y = targets[1][:, None, :, None] - source_pts[1][:, :, None, :]
        delta_z = targets[2][:, None, :, None] - source_pts[2][:, :, None, :]
        dist_sq = delta_x * delta_x + delta_y * delta_y + delta_z * delta_z
        kernel = (kernel_scale * lax.rsqrt(dist_sq + delta_sq)).astype(jnp.bfloat16)
        values = jnp.take(x_leaf, col_ids, axis=1)
        return jnp.einsum('gkpq,vgkq->gvp', kernel.astype(jnp.float32), values.astype(jnp.float32), precision=highest)
    own_pts = coords.reshape(3, groups, group_size, LEAF).transpose(1, 0, 2, 3)
    grouped = lax.map(near_group, (near_cols.reshape(groups, group_size, NEAR), own_pts))
    near_sum = grouped.reshape(LEAVES, NV, LEAF).transpose(1, 0, 2)
    return (near_sum + far_part).reshape(NV, POINTS)
```

```python
import functools

import jax
import jax.numpy as jnp
from jax import lax
from jax.experimental import pallas as pl
from jax.experimental.pallas import tpu as pltpu
from jax.sharding import PartitionSpec as P

F32 = jnp.float32
BF16 = jnp.bfloat16
REACH = 8
KERNEL_SCALE = 1.0 / 64.0
DELTA_SQ = 0.0025

GROUP = 8
GROUP_BITS = 3


def _spec(space=pltpu.VMEM):
    return pl.BlockSpec(memory_space=space)


def _call(body, outs, n_in, smem=(), scratch=(), flops=0, name=None):
    return pl.pallas_call(
        body,
        out_shape=outs,
        in_specs=[_spec(pltpu.SMEM) if i in smem else _spec() for i in range(n_in)],
        out_specs=jax.tree.map(lambda _: _spec(), outs),
        scratch_shapes=list(scratch),
        compiler_params=pltpu.CompilerParams(vmem_limit_bytes=40 * 1024 * 1024),
        cost_estimate=pl.CostEstimate(flops=flops, bytes_accessed=1 << 20, transcendentals=0),
        name=name,
    )


def _shape(shape, dtype):
    return jax.ShapeDtypeStruct(shape, dtype)


def _dot(a, b):
    return jnp.dot(a, b, preferred_element_type=F32)


def _dot_t(a, b):
    return lax.dot_general(a, b, (((1,), (1,)), ((), ())), preferred_element_type=F32)


def _leading(c):
    p = c * 65537.0
    return p - (p - c)


def _two(c):
    high = _leading(c)
    return jnp.concatenate([high, c - high], axis=0).astype(BF16)


def _mul(c, w):
    rows = c.shape[0]
    both = _dot(_two(c), w)
    return both[:rows] + both[rows:]


def _mul_t(c, w):
    rows = c.shape[0]
    both = _dot_t(_two(c), w)
    return both[:rows] + both[rows:]


def _swap_halves(x):
    half = x.shape[-1] // 2
    return jnp.concatenate([x[:, half:], x[:, :half]], axis=1)


def _request_kernel(anchor_ref, leaves_ref, table_ref, plan_ref):
    me = lax.axis_index("leaf")
    pairs = anchor_ref.shape[1]
    tiles = leaves_ref.shape[0]
    del tiles
    anchor = anchor_ref[...]
    source = leaves_ref[0:1, :]
    my_z = me // GROUP
    my_k = me % GROUP
    core = anchor & 1
    dz = ((anchor >> GROUP_BITS) - my_z) & 7
    near_side = (dz & 3) == 0
    server = jnp.where(near_side, core, jnp.where(dz > 4, 0, 1))
    step = jnp.where(dz > 4, 8 - dz, dz)
    base = jnp.where(
        dz == 0,
        0,
        jnp.where(dz == 4, 224, 32 + (step - 1) * 64 + (core ^ server) * 32),
    )
    tile = base + (source >> 1)
    group = (((anchor & 6) | server) ^ my_k)
    sub8 = lax.broadcasted_iota(jnp.int32, (8, pairs), 0)
    picked = (sub8 == group).astype(F32)
    row = lax.broadcasted_iota(jnp.int32, (pairs, pairs), 0)
    col = lax.broadcasted_iota(jnp.int32, (pairs, pairs), 1)
    upto = (row <= col).astype(F32).astype(BF16)
    count = _dot(picked.astype(BF16), upto)
    slot = (jnp.sum(picked * count, axis=0, keepdims=True) - 1.0).astype(jnp.int32)
    flip = (source ^ slot) & 1
    sub128 = lax.broadcasted_iota(jnp.int32, (128, pairs), 0)
    placed = (sub128 == slot).astype(F32).astype(BF16)
    table = _dot_t((picked * tile.astype(F32)).astype(BF16), placed)
    flips = _dot_t((picked * flip.astype(F32)).astype(BF16), placed)
    table_ref[...] = table + 256.0 * flips
    place = group * 64 + slot
    number = lax.broadcasted_iota(jnp.int32, (1, pairs), 1)
    plan_ref[0:1, :] = (place >> 1) + 256 * ((place ^ number) & 1)
    plan_ref[1:2, :] = leaves_ref[1:2, :]


def _coeff_kernel(vec_ref, basis_ref, sent_ref, coeff_ref):
    leaves = basis_ref.shape[0]
    lane = lax.broadcasted_iota(jnp.int32, (16, 128), 1)
    for i in range(leaves // 2):
        x0 = vec_ref[:, 256 * i : 256 * i + 128]
        x1 = vec_ref[:, 256 * i + 128 : 256 * i + 256]
        w = basis_ref[2 * i : 2 * i + 2].reshape(128, 128)
        r = _dot_t(jnp.concatenate([x0, x1], axis=0), w)
        c = jnp.where(lane < 64, r[:16], r[16:])
        coeff_ref[i] = c
        sent_ref[i] = c.astype(BF16)


def _up_kernel(coeff_ref, move_ref, table_ref, levels_ref, out_ref):
    def parent(tile, node):
        return _mul(tile, move_ref[node : node + 2].reshape(128, 64))

    size = 32
    current = [coeff_ref[i] for i in range(size)]
    node = 64
    while True:
        parents = [parent(current[i], node + 2 * i) for i in range(size)]
        if size == 1:
            root = parents[0]
            break
        size //= 2
        node //= 2
        current = [
            jnp.concatenate([parents[2 * i], parents[2 * i + 1]], axis=1) for i in range(size)
        ]
        for i in range(size):
            levels_ref[size + i] = current[i]
    levels_ref[0] = jnp.concatenate([root, root], axis=1)
    out_ref[0:8, :] = table_ref[...]
    out_ref[8:24, :] = jnp.concatenate([root, _mul(root, move_ref[1])], axis=1)


def _pair(a, b):
    return jnp.concatenate([a, b], axis=1)


def _group_kernel(group_ref, upper_ref, sib_ref, top_ref):
    me = lax.axis_index("leaf")
    my_k = me % GROUP
    my_z = me // GROUP
    shares = [group_ref[a ^ my_k, 8:24, 64:128] for a in range(GROUP)]
    sib_ref[0] = group_ref[1, 8:24, 0:64]
    nodes = [shares[2 * i] + shares[2 * i + 1] for i in range(GROUP // 2)]
    depth = 1
    while len(nodes) > 1:
        want = (my_k >> depth) ^ 1
        sib = nodes[0]
        for i in range(1, len(nodes)):
            sib = jnp.where(want == i, nodes[i], sib)
        sib_ref[depth] = sib
        depth += 1
        first = (GROUP + my_z) * len(nodes)
        nodes = [
            _mul(
                _pair(nodes[2 * i], nodes[2 * i + 1]),
                upper_ref[pl.ds(first + 2 * i, 2)].reshape(128, 64),
            )
            for i in range(len(nodes) // 2)
        ]
    top_ref[...] = nodes[0]


def _tree_kernel(
    coeff_ref, levels_ref, sib_ref, planes_ref, move_ref, pair_ref, upper_t_ref, upper_c_ref, out_ref
):
    me = lax.axis_index("leaf")
    my_z = me // GROUP
    sibs = [sib_ref[0], sib_ref[1], sib_ref[2], planes_ref[1]]
    nodes = [planes_ref[a ^ my_z] for a in range(8)]
    two = [
        _mul(
            _pair(nodes[2 * i], nodes[2 * i + 1]),
            upper_t_ref[8 + 2 * i : 10 + 2 * i].reshape(128, 64),
        )
        for i in range(4)
    ]
    want = (my_z >> 1) ^ 1
    sib = jnp.zeros((16, 64), F32)
    for i in range(4):
        sib = jnp.where(want == i, two[i], sib)
    sibs.append(sib)
    one = [
        _mul(_pair(two[2 * i], two[2 * i + 1]), upper_t_ref[4 + 2 * i : 6 + 2 * i].reshape(128, 64))
        for i in range(2)
    ]
    sibs.append(jnp.where((my_z >> 2) == 0, one[1], one[0]))
    node = 64 + me
    local = None
    for depth in range(1, 7):
        bit = 6 - depth
        if bit == 0:
            move, pair = move_ref[1], pair_ref[1]
        else:
            move, pair = upper_t_ref[node >> bit], upper_c_ref[node >> bit]
        coupled = _mul(sibs[bit], pair)
        local = coupled if local is None else _mul_t(local, move) + coupled
    lane = lax.broadcasted_iota(jnp.int32, (16, 128), 1)
    parents = [local]
    size = 1
    while True:
        children = []
        for i in range(size):
            node = 2 * size + 2 * i
            tile = coeff_ref[i] if size == 32 else levels_ref[size + i]
            moved = _mul_t(parents[i], move_ref[node : node + 2].reshape(128, 64))
            w = pair_ref[node : node + 2].reshape(128, 64)
            other = _swap_halves(tile)
            both = _mul(
                jnp.concatenate(
                    [jnp.where(lane < 64, other, 0.0), jnp.where(lane < 64, 0.0, other)], axis=0
                ),
                w,
            )
            children.append(moved + _pair(both[:16], both[16:]))
        if size == 32:
            break
        parents = []
        for c in children:
            parents += [c[:, :64], c[:, 64:]]
        size *= 2
    for i in range(32):
        out_ref[i] = children[i]


def _both_ways(scratch, blocks):
    at = 0
    for ref in blocks:
        count = ref.shape[0]
        x = ref[...]
        scratch[at : at + count] = x
        y = _swap_halves(x.reshape(count * 16, 128)).reshape(count, 16, 128)
        scratch[256 + at : 256 + at + count] = y
        at += count


def _gather_kernel(table_ref, b0, b1, b2, b3, b4, *rest):
    outs, scratch = rest[:GROUP], rest[GROUP]
    _both_ways(scratch, [b0, b1, b2, b3, b4])
    lane = lax.broadcasted_iota(jnp.int32, (16, 128), 1)
    for k in range(GROUP):
        for s in range(32):
            a = scratch[table_ref[k, 2 * s]]
            b = scratch[table_ref[k, 2 * s + 1]]
            outs[k][s] = jnp.where(lane < 64, a, b)


def _points_kernel(p0, p1, p2, p3, vec_ref, source_ref, target_ref, first_ref, last_ref):
    mine = lax.axis_index("vec")
    width = p0.shape[1]
    for shift, ref in enumerate((p0, p1, p2, p3)):
        spot = pl.multiple_of(((mine + shift) & 3) * width, width)
        c = ref[...] - 0.5
        high = _leading(c)
        mid = _leading(c - high)
        rounded = high + mid
        square = rounded * rounded
        norm = square[0:1] + square[1:2] + square[2:3]

        def thirds(n):
            n1 = _leading(n)
            n2 = _leading(n - n1)
            return [n1, n2, n - n1 - n2]

        one = jnp.ones((3, width), F32)
        zero = jnp.zeros((2, width), F32)
        own = jnp.concatenate([high, mid, zero], axis=0)
        source = jnp.concatenate([own, jnp.concatenate(thirds(norm + DELTA_SQ) + [one, zero], axis=0)], axis=0)
        target = jnp.concatenate(
            [
                -2.0 * jnp.concatenate([high, high, zero], axis=0),
                -2.0 * jnp.concatenate([mid, mid, zero], axis=0),
                jnp.concatenate([one] + thirds(norm) + [zero], axis=0),
                jnp.zeros((8, width), F32),
            ],
            axis=0,
        )
        source_ref[:, pl.ds(spot, width)] = source.astype(BF16)
        target_ref[:, pl.ds(spot, width)] = target.astype(BF16)
    halo = first_ref.shape[1]
    total = vec_ref.shape[1]
    first_ref[0:16, :] = source_ref[:, 0:halo]
    first_ref[16:32, :] = vec_ref[:, 0:halo]
    last_ref[0:16, :] = source_ref[:, total - halo : total]
    last_ref[16:32, :] = vec_ref[:, total - halo : total]


def _near_kernel(cols_ref, source_ref, target_ref, vec_ref, left_ref, right_ref, out_ref, rows, values):
    me = lax.axis_index("leaf")
    leaves = cols_ref.shape[1]
    first = REACH - me * leaves
    zero = jnp.zeros((8, 128), F32)

    def place(index, feature, value):
        f = feature.astype(F32)
        f = jnp.concatenate([f[0:8], f[0:8], f[8:16], zero], axis=0)
        rows[index] = jnp.transpose(f).astype(BF16)
        values[index] = value

    for i in range(REACH):
        lanes = slice(128 * i, 128 * i + 128)
        place(i, left_ref[0:16, lanes], left_ref[16:32, lanes])
        place(REACH + leaves + i, right_ref[0:16, lanes], right_ref[16:32, lanes])
    for i in range(leaves):
        lanes = slice(128 * i, 128 * i + 128)
        place(REACH + i, source_ref[:, lanes], vec_ref[:, lanes])

    def leaf(t, carry):
        lanes = pl.ds(pl.multiple_of(t * 128, 128), 128)
        target = target_ref[:, lanes]
        kernel, value = [], []
        for k in range(cols_ref.shape[0]):
            index = cols_ref[k, t] + first
            dist = _dot(rows[index], target)
            kernel.append(lax.rsqrt(dist).astype(BF16))
            value.append(values[index])
        total = _dot(jnp.concatenate(value, axis=1), jnp.concatenate(kernel, axis=0))
        out_ref[:, lanes] = total * KERNEL_SCALE
        return carry

    lax.fori_loop(0, leaves, leaf, 0, unroll=2)


def _final_kernel(plan_ref, r0, r1, r2, r3, r4, r5, r6, r7, block_ref, local_ref, basis_ref, near_ref, out_ref, scratch, far):
    _both_ways(scratch, [r0, r1, r2, r3, r4, r5, r6, r7])
    far[...] = jnp.zeros_like(far)
    lane = lax.broadcasted_iota(jnp.int32, (16, 128), 1)
    pairs = block_ref.shape[0]

    def add(i, carry):
        w = block_ref[pl.ds(2 * i, 2)].reshape(128, 64)
        a = scratch[plan_ref[0, 2 * i]]
        b = scratch[plan_ref[0, 2 * i + 1]]
        zero = jnp.zeros_like(a)
        x = jnp.concatenate([jnp.where(lane < 64, a, zero), jnp.where(lane < 64, zero, b)], axis=0)
        r = _dot(x, w)
        far[plan_ref[1, 2 * i]] += r[:16]
        far[plan_ref[1, 2 * i + 1]] += r[16:]
        return carry

    lax.fori_loop(0, pairs // 2, add, 0, unroll=4)
    for i in range(basis_ref.shape[0] // 2):
        total = (local_ref[i] + _pair(far[2 * i], far[2 * i + 1])).astype(BF16)
        zero = jnp.zeros_like(total)
        x = jnp.concatenate([jnp.where(lane < 64, total, zero), jnp.where(lane < 64, zero, total)], axis=0)
        r = _dot(x, basis_ref[2 * i : 2 * i + 2].reshape(128, 128))
        at = 256 * i
        out_ref[:, at : at + 128] = near_ref[:, at : at + 128] + r[:16]
        out_ref[:, at + 128 : at + 256] = near_ref[:, at + 128 : at + 256] + r[16:]


def per_device(
    vectors,
    points,
    leaf_basis,
    local_transfer,
    local_coupling,
    upper_transfer,
    upper_coupling,
    far_anchor,
    far_leaves,
    far_block,
    near_cols,
):
    n_leaf = lax.axis_size("leaf")
    n_vec = lax.axis_size("vec")
    everyone = range(n_leaf)

    def permute(x, to):
        return lax.ppermute(x, "leaf", [(i, to(i)) for i in everyone])

    tile = (32, 16, 128)

    table, plan = _call(
        _request_kernel,
        [_shape((8, 128), F32), _shape((2, 256), jnp.int32)],
        2,
        flops=1 << 20,
        name="request",
    )(far_anchor.reshape(1, -1), far_leaves.T)

    sent, coeff = _call(
        _coeff_kernel, [_shape(tile, BF16), _shape(tile, F32)], 2, flops=1 << 24, name="coeff"
    )(vectors, leaf_basis)

    def onward(i):
        z, rest = i // GROUP, i % GROUP
        return (z + 1 if i % 2 == 0 else z - 1) % (n_leaf // GROUP) * GROUP + rest

    mate = permute(sent, lambda i: i ^ 1)
    ring1 = permute(jnp.concatenate([sent, mate], axis=0), onward)
    ring2 = permute(ring1, onward)
    ring3 = permute(ring2, onward)
    ring4 = permute(ring3[:32], onward)

    levels, carried = _call(
        _up_kernel, [_shape(tile, F32), _shape((24, 128), F32)], 3, flops=1 << 24, name="up"
    )(coeff, local_transfer, table)
    group = carried[None]
    for bit in range(GROUP_BITS):
        group = jnp.concatenate([group, permute(group, lambda i: i ^ (1 << bit))], axis=0)
    siblings, top = _call(
        _group_kernel, [_shape((3, 16, 64), F32), _shape((16, 64), F32)], 2, flops=1 << 20, name="group"
    )(group, upper_transfer)
    planes = top[None]
    for bit in range(GROUP_BITS):
        planes = jnp.concatenate([planes, permute(planes, lambda i: i ^ (GROUP << bit))], axis=0)

    wanted = jnp.stack([group[k, k] for k in range(GROUP)]).astype(jnp.int32)
    rows = _call(
        _gather_kernel,
        [_shape(tile, BF16)] * GROUP,
        6,
        smem=(0,),
        scratch=[pltpu.VMEM((512, 16, 128), BF16)],
        flops=1 << 22,
        name="gather",
    )(wanted, sent, ring1, ring2, ring3, ring4)
    got = [rows[0]] + [permute(rows[k], lambda i, k=k: i ^ k) for k in range(1, GROUP)]

    turns = [points] + [
        lax.ppermute(points, "vec", [((i + s) % n_vec, i) for i in range(n_vec)]) for s in range(1, n_vec)
    ]
    halo = REACH * leaf_basis.shape[2]
    width = vectors.shape[1]
    source, target, first, last = _call(
        _points_kernel,
        [
            _shape((16, width), BF16),
            _shape((32, width), BF16),
            _shape((32, halo), BF16),
            _shape((32, halo), BF16),
        ],
        5,
        flops=1 << 22,
        name="points",
    )(*turns, vectors)
    left = lax.ppermute(last, "leaf", [(i, i + 1) for i in range(n_leaf - 1)])
    right = lax.ppermute(first, "leaf", [(i + 1, i) for i in range(n_leaf - 1)])
    blocks = leaf_basis.shape[0] + 2 * REACH
    near = _call(
        _near_kernel,
        _shape(vectors.shape, F32),
        6,
        smem=(0,),
        scratch=[pltpu.VMEM((blocks, 128, 32), BF16), pltpu.VMEM((blocks, 16, 128), BF16)],
        flops=1 << 30,
        name="near",
    )(near_cols.T, source, target, vectors, left, right)

    local = _call(_tree_kernel, _shape(tile, F32), 8, flops=1 << 26, name="tree")(
        coeff, levels, siblings, planes, local_transfer, local_coupling, upper_transfer, upper_coupling
    )
    return _call(
        _final_kernel,
        _shape(vectors.shape, F32),
        13,
        smem=(0,),
        scratch=[pltpu.VMEM((512, 16, 128), BF16), pltpu.VMEM((64, 16, 64), F32)],
        flops=1 << 27,
        name="final",
    )(plan, *got, far_block, local, leaf_basis, near)


def solution(mesh):
    return jax.shard_map(
        per_device,
        mesh=mesh,
        in_specs=(
            P("vec", "leaf"),
            P(None, ("leaf", "vec")),
            P("leaf", None, None),
            P("leaf", None, None),
            P("leaf", None, None),
            P(),
            P(),
            P("leaf", None),
            P("leaf", None),
            P("leaf", None, None),
            P("leaf", None),
        ),
        out_specs=P("vec", "leaf"),
        check_vma=False,
    )
```

```python
import functools

import jax
import jax.numpy as jnp
from jax import lax
from jax.experimental import pallas as pl
from jax.experimental.layout import Layout, with_layout_constraint
from jax.experimental.pallas import tpu as pltpu
from jax.sharding import PartitionSpec as P

F32 = jnp.float32
BF16 = jnp.bfloat16
REACH = 8
KERNEL_SCALE = 1.0 / 64.0
DELTA_SQ = 0.0025

GROUP = 8
GROUP_BITS = 3

NEAR_PARTS = 2


def _spec(space=pltpu.VMEM):
    return pl.BlockSpec(memory_space=space)


def _call(body, outs, n_in, smem=(), scratch=(), flops=0, name=None, mib=8, hbm=()):
    return pl.pallas_call(
        body,
        out_shape=outs,
        in_specs=[
            _spec(pltpu.SMEM if i in smem else pltpu.HBM if i in hbm else pltpu.VMEM) for i in range(n_in)
        ],
        out_specs=jax.tree.map(lambda _: _spec(), outs),
        scratch_shapes=list(scratch),
        compiler_params=pltpu.CompilerParams(vmem_limit_bytes=mib * 1024 * 1024),
        cost_estimate=pl.CostEstimate(flops=flops, bytes_accessed=1 << 20, transcendentals=0),
        name=name,
    )


def _shape(shape, dtype):
    return jax.ShapeDtypeStruct(shape, dtype)


def _dot(a, b):
    return jnp.dot(a, b, preferred_element_type=F32)


def _dot_t(a, b):
    return lax.dot_general(a, b, (((1,), (1,)), ((), ())), preferred_element_type=F32)


def _leading(c):
    p = c * 65537.0
    return p - (p - c)


def _two(c):
    high = _leading(c)
    return jnp.concatenate([high, c - high], axis=0).astype(BF16)


def _mul(c, w):
    rows = c.shape[0]
    both = _dot(_two(c), w)
    return both[:rows] + both[rows:]


def _mul_t(c, w):
    rows = c.shape[0]
    both = _dot_t(_two(c), w)
    return both[:rows] + both[rows:]


def _swap_halves(x):
    half = x.shape[-1] // 2
    return jnp.concatenate([x[:, half:], x[:, :half]], axis=1)


def _pair(a, b):
    return jnp.concatenate([a, b], axis=1)


def _request(anchor_ref, leaves_ref, plan_ref):
    me = lax.axis_index("leaf")
    pairs = anchor_ref.shape[1]
    anchor = anchor_ref[...]
    source = leaves_ref[0:1, :]
    my_z = me // GROUP
    my_k = me % GROUP
    core = anchor & 1
    dz = ((anchor >> GROUP_BITS) - my_z) & 7
    near_side = (dz & 3) == 0
    server = jnp.where(near_side, core, jnp.where(dz > 4, 0, 1))
    step = jnp.where(dz > 4, 8 - dz, dz)
    base = jnp.where(
        dz == 0,
        0,
        jnp.where(dz == 4, 224, 32 + (step - 1) * 64 + (core ^ server) * 32),
    )
    tile = base + (source >> 1)
    group = (((anchor & 6) | server) ^ my_k)
    sub8 = lax.broadcasted_iota(jnp.int32, (8, pairs), 0)
    picked = (sub8 == group).astype(F32)
    row = lax.broadcasted_iota(jnp.int32, (pairs, pairs), 0)
    col = lax.broadcasted_iota(jnp.int32, (pairs, pairs), 1)
    upto = (row <= col).astype(F32).astype(BF16)
    count = _dot(picked.astype(BF16), upto)
    slot = (jnp.sum(picked * count, axis=0, keepdims=True) - 1.0).astype(jnp.int32)
    flip = (source ^ slot) & 1
    sub128 = lax.broadcasted_iota(jnp.int32, (128, pairs), 0)
    placed = (sub128 == slot).astype(F32).astype(BF16)
    table = _dot_t((picked * tile.astype(F32)).astype(BF16), placed)
    flips = _dot_t((picked * flip.astype(F32)).astype(BF16), placed)
    halves = jnp.floor((count[:, pairs - 1 : pairs] + 1.0) * 0.5)
    before = jnp.sum(jnp.where(sub8 < group, halves, 0.0), axis=0, keepdims=True)
    position = before.astype(jnp.int32) + (slot >> 1)
    even = (slot & 1) == 0
    number = lax.broadcasted_iota(jnp.int32, (1, pairs), 1)
    wanted = leaves_ref[1:2, :]

    def only(which, value):
        return jnp.where(which, value, 0).astype(F32)

    odd = jnp.logical_not(even)
    facts = jnp.concatenate(
        [
            only(even, group * 32 + (slot >> 1)),
            only(even, number),
            only(odd, number),
            only(even, wanted),
            only(odd, wanted),
            only(even, jnp.ones_like(slot)),
            only(odd, jnp.ones_like(slot)),
            jnp.zeros((1, pairs), F32),
        ],
        axis=0,
    )
    listed = (row == position).astype(F32).astype(BF16)
    plan = _dot_t(facts.astype(BF16), listed)
    plan_ref[0:3, :] = plan[0:3].astype(jnp.int32)
    plan_ref[3:4, :] = (plan[3:4] + 64.0 * (1.0 - plan[5:6])).astype(jnp.int32)
    plan_ref[4:5, :] = (plan[4:5] + 64.0 * (1.0 - plan[6:7])).astype(jnp.int32)
    total = jnp.sum(halves, axis=0, keepdims=True)
    plan_ref[5:8, :] = jnp.broadcast_to(total, (3, pairs)).astype(jnp.int32)
    return jnp.concatenate([table, flips], axis=0).astype(BF16)


LEAF_TILES = 32
OWN_TILES = LEAF_TILES + 1
TABLE_AT = OWN_TILES
EDGE_AT = TABLE_AT + 1
MATE_TILES = EDGE_AT + 2 * REACH


def _split_points(coords):
    c = coords - 0.5
    high = _leading(c)
    return high, _leading(c - high)


def _prepare_kernel(
    anchor_ref, leaves_ref, vec_ref, basis_ref, move_ref, p0, p1, p2, p3,
    own_ref, give_ref, edge_ref, coeff_ref, levels_ref, plan_ref,
):
    me = lax.axis_index("leaf")
    mine = lax.axis_index("vec")
    core = me & 1
    leaves = basis_ref.shape[0]
    lane = lax.broadcasted_iota(jnp.int32, (16, 128), 1)

    current = []
    for i in range(leaves // 2):
        x0 = vec_ref[:, 256 * i : 256 * i + 128]
        x1 = vec_ref[:, 256 * i + 128 : 256 * i + 256]
        w = basis_ref[2 * i : 2 * i + 2].reshape(128, 128)
        r = _dot_t(jnp.concatenate([x0, x1], axis=0), w)
        c = jnp.where(lane < 64, r[:16], r[16:])
        coeff_ref[i] = c
        own_ref[i] = c.astype(BF16)
        give_ref[i] = c.astype(BF16)
        current.append(c)

    size, node = leaves // 2, leaves
    while True:
        parents = [
            _mul(current[i], move_ref[node + 2 * i : node + 2 * i + 2].reshape(128, 64))
            for i in range(size)
        ]
        if size == 1:
            root = parents[0]
            break
        size //= 2
        node //= 2
        current = [_pair(parents[2 * i], parents[2 * i + 1]) for i in range(size)]
        for i in range(size):
            levels_ref[size + i] = current[i]
    levels_ref[0] = jnp.zeros((16, 128), F32)
    passed = _pair(_mul(root, move_ref[1]), root).astype(BF16)
    own_ref[LEAF_TILES] = passed
    give_ref[LEAF_TILES] = passed

    give_ref[TABLE_AT] = _request(anchor_ref, leaves_ref, plan_ref)

    width = p0.shape[1]
    halo = REACH * 128

    def end(last):
        block, lanes = (3, slice(width - halo, width)) if last else (0, slice(0, halo))
        chosen = p0[:, lanes]
        for turn, ref in ((1, p1), (2, p2), (3, p3)):
            chosen = jnp.where(((mine + turn) & 3) == block, ref[:, lanes], chosen)
        return chosen

    def place(ref, at, coords, first):
        high, mid = _split_points(coords)
        both = jnp.concatenate([high, mid, jnp.zeros((10, halo), F32)], axis=0).astype(BF16)
        for j in range(REACH):
            lanes = pl.ds(pl.multiple_of((first + j) * 128, 128), 128)
            ref[at + j] = vec_ref[:, lanes]
            ref[at + REACH + j] = both[:, 128 * j : 128 * j + 128]

    low, high = end(False), end(True)
    place(give_ref, EDGE_AT, jnp.where(core == 0, high, low), jnp.where(core == 0, leaves - REACH, 0))
    place(edge_ref, 0, jnp.where(core == 0, low, high), jnp.where(core == 0, 0, leaves - REACH))


def _inner_kernel(coeff_ref, levels_ref, move_ref, pair_ref, out_ref, couple_ref):
    lane = lax.broadcasted_iota(jnp.int32, (16, 128), 1)
    couple_ref[...] = pair_ref[1]
    parents = None
    size = 1
    while True:
        children = []
        for i in range(size):
            node = 2 * size + 2 * i
            tile = coeff_ref[i] if size == LEAF_TILES else levels_ref[size + i]
            other = _swap_halves(tile)
            both = _mul(
                jnp.concatenate(
                    [jnp.where(lane < 64, other, 0.0), jnp.where(lane < 64, 0.0, other)], axis=0
                ),
                pair_ref[node : node + 2].reshape(128, 64),
            )
            child = _pair(both[:16], both[16:])
            if parents is not None:
                child = child + _mul_t(parents[i], move_ref[node : node + 2].reshape(128, 64))
            children.append(child)
        if size == LEAF_TILES:
            break
        parents = []
        for c in children:
            parents += [c[:, :64], c[:, 64:]]
        size *= 2
    for i in range(LEAF_TILES):
        out_ref[i] = children[i]


def _from_root(root_local, move_ref):
    parents = [root_local]
    size = 1
    while True:
        children = [
            _mul_t(parents[i], move_ref[2 * size + 2 * i : 2 * size + 2 * i + 2].reshape(128, 64))
            for i in range(size)
        ]
        if size == LEAF_TILES:
            return children
        parents = []
        for c in children:
            parents += [c[:, :64], c[:, 64:]]
        size *= 2


def _root_local(mate_passed, got, move_ref, couple_ref, upper_t_ref, upper_c_ref, c5, c4, c3, c2, c1):
    me = lax.axis_index("leaf")
    my_k = me % GROUP
    my_z = me // GROUP
    my_x = my_k >> 1

    def chip(x, c, tile):
        return got[(2 * x + c) ^ my_k, tile].astype(F32)

    for x in range(4):
        c5[my_z * 4 + x] = chip(x, 0, 0)[:, 0:64]
        for c, sign in ((0, -1), (1, 1)):
            one, two = chip(x, c, 0), chip(x, c, 1)
            steps = [one[:, 64:128], two[:, 0:64], two[:, 64:128]]
            for i in range(3):
                c5[((my_z + sign * (i + 1)) & 7) * 4 + x] = steps[i]
        c5[((my_z + 4) & 7) * 4 + x] = chip(x, 0, 2)[:, 0:64] + chip(x, 1, 2)[:, 0:64]
    count = 32
    for below, above in ((c5, c4), (c4, c3), (c3, c2), (c2, c1)):
        for i in range(count // 2):
            node = count + 2 * i
            above[i] = _mul(
                _pair(below[2 * i], below[2 * i + 1]), upper_t_ref[node : node + 2].reshape(128, 64)
            )
        count //= 2
    place = my_z * 4 + my_x
    sibs = [
        mate_passed[:, 64:128].astype(F32),
        c5[place ^ 1],
        c4[(place >> 1) ^ 1],
        c3[(place >> 2) ^ 1],
        c2[(place >> 3) ^ 1],
        c1[(place >> 4) ^ 1],
    ]
    node = 64 + me
    coupled = [_mul(sibs[bit], upper_c_ref[node >> bit] if bit else couple_ref[...]) for bit in range(6)]
    local = coupled[5]
    for bit in range(4, -1, -1):
        local = _mul_t(local, upper_t_ref[node >> bit] if bit else move_ref[1]) + coupled[bit]
    return local


def _tree_kernel(
    pair_in, g0, g1, g2, g3, g4, g5, g6, g7, inner_ref, move_ref, couple_ref, upper_t_ref, upper_c_ref,
    out_ref, got, c5, c4, c3, c2, c1,
):
    for k, ref in enumerate((g0, g1, g2, g3, g4, g5, g6, g7)):
        got[k] = ref[LEAF_TILES : LEAF_TILES + 3]
    root_local = _root_local(
        pair_in[OWN_TILES + LEAF_TILES], got, move_ref, couple_ref, upper_t_ref, upper_c_ref, c5, c4, c3, c2, c1
    )
    down = _from_root(root_local, move_ref)
    for i in range(LEAF_TILES):
        out_ref[i] = inner_ref[i] + down[i]


def _both_ways(scratch, blocks):
    at = 0
    for ref, first in blocks:
        x = ref[first : first + LEAF_TILES]
        scratch[at : at + LEAF_TILES] = x
        y = _swap_halves(x.reshape(LEAF_TILES * 16, 128)).reshape(LEAF_TILES, 16, 128)
        scratch[256 + at : 256 + at + LEAF_TILES] = y
        at += LEAF_TILES


def _gather_kernel(table_ref, pair, r1, r2, r3, r4, *rest):
    outs, scratch = rest[:GROUP], rest[GROUP]
    blocks = [(pair, 0)]
    for ref in (r1, r2, r3):
        blocks += [(ref, 0), (ref, OWN_TILES)]
    _both_ways(scratch, blocks + [(r4, 0)])
    lane = lax.broadcasted_iota(jnp.int32, (16, 128), 1)

    def chip(ref):
        return (ref[LEAF_TILES].astype(F32) + ref[OWN_TILES + LEAF_TILES].astype(F32))[:, :64]

    passed = [
        _pair(chip(pair), chip(r1)).astype(BF16),
        _pair(chip(r2), chip(r3)).astype(BF16),
        r4[LEAF_TILES],
    ]
    for k in range(GROUP):
        for s in range(LEAF_TILES):
            a = scratch[table_ref[k, 2 * s]]
            b = scratch[table_ref[k, 2 * s + 1]]
            outs[k][s] = jnp.where(lane < 64, a, b)
        for i in range(3):
            outs[k][LEAF_TILES + i] = passed[i]


def _features(high, mid):
    width = high.shape[1]
    rounded = high + mid
    square = rounded * rounded
    norm = square[0:1] + square[1:2] + square[2:3]

    def thirds(n):
        n1 = _leading(n)
        n2 = _leading(n - n1)
        return [n1, n2, n - n1 - n2]

    one = jnp.ones((3, width), F32)
    zero = jnp.zeros((2, width), F32)
    pad = jnp.zeros((8, width), F32)
    own = [high, mid, zero]
    source = jnp.concatenate(own + own + thirds(norm + DELTA_SQ) + [one, zero, pad], axis=0)
    target = jnp.concatenate(
        [-2.0 * high, -2.0 * high, zero, -2.0 * mid, -2.0 * mid, zero, one] + thirds(norm) + [zero, pad],
        axis=0,
    )
    return source, target


TOGETHER = 8


def _near_kernel(
    part, parts, cols_ref, p0, p1, p2, p3, vec_ref, mate_ref, edge_ref, out_ref, rows, values, targets, kernel
):
    me = lax.axis_index("leaf")
    mine = lax.axis_index("vec")
    core = me & 1
    leaves = cols_ref.shape[1]
    near, count = cols_ref.shape[0], leaves // parts
    begin = part * count
    per = p0.shape[1] // 128

    beyond = jnp.where(core == 0, REACH + leaves, 0)
    for ref, first, at in ((mate_ref, EDGE_AT, beyond), (edge_ref, 0, REACH + leaves - beyond)):
        for j in range(REACH):
            both = ref[first + REACH + j].astype(F32)
            features = _features(both[0:3], both[3:6])[0]
            rows[at + j] = jnp.transpose(features).astype(BF16)
            values[at + j] = ref[first + j]
    for turn, ref in enumerate((p0, p1, p2, p3)):
        block = (mine + turn) & 3
        features, target = _features(*_split_points(ref[...]))
        for j in range(per):
            at = block * per + j
            rows[REACH + at] = jnp.transpose(features[:, 128 * j : 128 * j + 128]).astype(BF16)
            targets[at] = target[:, 128 * j : 128 * j + 128].astype(BF16)
    for i in range(leaves):
        values[REACH + i] = vec_ref[:, 128 * i : 128 * i + 128]

    shift = REACH - me * leaves

    def group(step, carry):
        for g in range(TOGETHER):
            t = begin + step * TOGETHER + g
            target = targets[t]
            for k in range(near):
                dist = _dot(rows[cols_ref[k, t] + shift], target)
                kernel[g, 128 * k : 128 * k + 128] = lax.rsqrt(dist).astype(BF16)
        for g in range(TOGETHER):
            t = begin + step * TOGETHER + g
            value = jnp.concatenate([values[cols_ref[k, t] + shift] for k in range(near)], axis=1)
            lanes = pl.ds(pl.multiple_of((step * TOGETHER + g) * 128, 128), 128)
            out_ref[:, lanes] = _dot(value, kernel[g]) * KERNEL_SCALE
        return carry

    lax.fori_loop(0, count // TOGETHER, group, 0)


BATCH = 8


def _final_kernel(plan_ref, r0, r1, r2, r3, r4, r5, r6, r7, block_ref, local_ref, basis_ref, *rest):
    nears, (out_ref, got, far) = rest[:NEAR_PARTS], rest[NEAR_PARTS:]
    for k, ref in enumerate((r0, r1, r2, r3, r4, r5, r6, r7)):
        got[32 * k : 32 * k + 32] = ref[0:LEAF_TILES]
    far[...] = jnp.zeros_like(far)
    lane = lax.broadcasted_iota(jnp.int32, (16, 128), 1)

    def split(x):
        zero = jnp.zeros_like(x)
        return jnp.concatenate([jnp.where(lane < 64, x, zero), jnp.where(lane < 64, zero, x)], axis=0)

    def add(step, carry):
        sums = []
        for i in range(BATCH):
            j = step * BATCH + i
            w = jnp.concatenate([block_ref[plan_ref[1, j]], block_ref[plan_ref[2, j]]], axis=0)
            sums.append(_dot(split(got[plan_ref[0, j]]), w))
        for i in range(BATCH):
            j = step * BATCH + i
            far[plan_ref[3, j]] += sums[i][:16]
            far[plan_ref[4, j]] += sums[i][16:]
        return carry

    lax.fori_loop(0, (plan_ref[5, 0] + BATCH - 1) // BATCH, add, 0)
    for i in range(basis_ref.shape[0] // 2):
        total = (local_ref[i] + _pair(far[2 * i], far[2 * i + 1])).astype(BF16)
        r = _dot(split(total), basis_ref[2 * i : 2 * i + 2].reshape(128, 128))
        at = 256 * i
        near_ref, off = nears[at // nears[0].shape[1]], at % nears[0].shape[1]
        out_ref[:, at : at + 128] = near_ref[:, off : off + 128] + r[:16]
        out_ref[:, at + 128 : at + 256] = near_ref[:, off + 128 : off + 256] + r[16:]


def per_device(
    vectors,
    points,
    leaf_basis,
    local_transfer,
    local_coupling,
    upper_transfer,
    upper_coupling,
    far_anchor,
    far_leaves,
    far_block,
    near_cols,
):
    n_leaf = lax.axis_size("leaf")
    n_vec = lax.axis_size("vec")
    everyone = range(n_leaf)

    def permute(x, to):
        return lax.ppermute(x, "leaf", [(i, to(i)) for i in everyone])

    def after(x, *done):
        return lax.optimization_barrier((x, done))[0]

    def tiles(count, dtype=BF16):
        return _shape((count, 16, 128), dtype)

    width = vectors.shape[1]
    leaves = leaf_basis.shape[0]

    turns = [points] + [
        lax.ppermute(points, "vec", [((i + s) % n_vec, i) for i in range(n_vec)]) for s in range(1, n_vec)
    ]

    own, give, edge, coeff, levels, plan = _call(
        _prepare_kernel,
        [
            tiles(OWN_TILES),
            tiles(MATE_TILES),
            tiles(2 * REACH),
            tiles(LEAF_TILES, F32),
            tiles(LEAF_TILES, F32),
            _shape((8, far_anchor.shape[0]), jnp.int32),
        ],
        9,
        flops=1 << 26,
        name="prepare",
    )(far_anchor.reshape(1, -1), far_leaves.T, vectors, leaf_basis, local_transfer, *turns)
    mate = permute(give, lambda i: i ^ 1)
    beyond = lax.ppermute(
        edge, "leaf", [(i, i - 1 + 2 * (i % 2)) for i in range(n_leaf) if 0 <= i - 1 + 2 * (i % 2) < n_leaf]
    )

    def onward(i):
        z, rest = i // GROUP, i % GROUP
        return (z + 1 if i % 2 == 0 else z - 1) % (n_leaf // GROUP) * GROUP + rest

    pair = jnp.concatenate([own, mate[:OWN_TILES]], axis=0)
    ring1 = permute(pair, onward)
    tables = jnp.concatenate([give[TABLE_AT : TABLE_AT + 1], mate[TABLE_AT : TABLE_AT + 1]], axis=0)
    for bit in range(1, GROUP_BITS):
        tables = jnp.concatenate([tables, permute(tables, lambda i: i ^ (1 << bit))], axis=0)
    wanted = jnp.stack([tables[k, k] + 256 * tables[k, 8 + k].astype(F32) for k in range(GROUP)])
    wanted = wanted.astype(jnp.int32)

    blocks = leaves + 2 * REACH

    def near_part(part, done):
        args = after((near_cols.T, *turns, vectors, mate, beyond), done)
        return _call(
            functools.partial(_near_kernel, part, NEAR_PARTS),
            _shape((vectors.shape[0], width // NEAR_PARTS), F32),
            8,
            smem=(0,),
            scratch=[
                pltpu.VMEM((blocks, 128, 32), BF16),
                pltpu.VMEM((blocks, 16, 128), BF16),
                pltpu.VMEM((leaves, 32, 128), BF16),
                pltpu.VMEM((TOGETHER, 1024, 128), BF16),
            ],
            flops=1 << 31,
            name="near%d" % part,
            mib=12,
        )(*args)

    def by_rows(x, done):
        return with_layout_constraint(after(x, done), Layout(major_to_minor=(0, 1, 2)))

    far_block = by_rows(far_block, pair)
    ring2 = permute(after(ring1, far_block), onward)
    local_coupling = by_rows(local_coupling, ring1)
    ring3 = permute(after(ring2, local_coupling), onward)
    near = [near_part(0, ring2)]
    ring4 = permute(after(ring3, near[0])[:OWN_TILES], onward)

    rows = _call(
        _gather_kernel,
        [tiles(LEAF_TILES + 3)] * GROUP,
        6,
        smem=(0,),
        scratch=[pltpu.VMEM((512, 16, 128), BF16)],
        flops=1 << 22,
        name="gather",
    )(wanted, pair, ring1, ring2, ring3, ring4)
    got = [rows[0]] + [permute(rows[k], lambda i, k=k: i ^ k) for k in range(1, GROUP)]

    near.append(near_part(1, rows[0]))
    inner, couple = _call(
        _inner_kernel,
        [tiles(LEAF_TILES, F32), _shape((64, 64), BF16)],
        4,
        flops=1 << 28,
        name="inner",
    )(*after((coeff, levels), rows[0]), local_transfer, local_coupling)

    local = _call(
        _tree_kernel,
        tiles(LEAF_TILES, F32),
        14,
        scratch=[pltpu.VMEM((GROUP, 3, 16, 128), BF16)] + [pltpu.VMEM((n, 16, 64), F32) for n in (32, 16, 8, 4, 2)],
        flops=1 << 26,
        name="tree",
    )(pair, *got, inner, local_transfer, couple, upper_transfer, upper_coupling)
    return _call(
        _final_kernel,
        _shape(vectors.shape, F32),
        12 + NEAR_PARTS,
        smem=(0,),
        scratch=[pltpu.VMEM((256, 16, 128), BF16), pltpu.VMEM((65, 16, 64), F32)],
        flops=1 << 27,
        name="final",
        mib=16,
    )(plan, *got, far_block, local, leaf_basis, *near)


def solution(mesh):
    return jax.shard_map(
        per_device,
        mesh=mesh,
        in_specs=(
            P("vec", "leaf"),
            P(None, ("leaf", "vec")),
            P("leaf", None, None),
            P("leaf", None, None),
            P("leaf", None, None),
            P(),
            P(),
            P("leaf", None),
            P("leaf", None),
            P("leaf", None, None),
            P("leaf", None),
        ),
        out_specs=P("vec", "leaf"),
        check_vma=False,
    )
```

```python
import functools

import jax
import jax.numpy as jnp
from jax import lax
from jax.experimental import pallas as pl
from jax.experimental.layout import Layout, with_layout_constraint
from jax.experimental.pallas import tpu as pltpu
from jax.sharding import PartitionSpec as P

F32 = jnp.float32
BF16 = jnp.bfloat16
REACH = 8
KERNEL_SCALE = 1.0 / 64.0
DELTA_SQ = 0.0025

GROUP = 8
GROUP_BITS = 3

NEAR_PARTS = 1


def _spec(space=pltpu.VMEM):
    return pl.BlockSpec(memory_space=space)


def _call(body, outs, n_in, smem=(), scratch=(), flops=0, name=None, mib=8, hbm=()):
    return pl.pallas_call(
        body,
        out_shape=outs,
        in_specs=[
            _spec(pltpu.SMEM if i in smem else pltpu.HBM if i in hbm else pltpu.VMEM) for i in range(n_in)
        ],
        out_specs=jax.tree.map(lambda _: _spec(), outs),
        scratch_shapes=list(scratch),
        compiler_params=pltpu.CompilerParams(vmem_limit_bytes=mib * 1024 * 1024),
        cost_estimate=pl.CostEstimate(flops=flops, bytes_accessed=1 << 20, transcendentals=0),
        name=name,
    )


def _shape(shape, dtype):
    return jax.ShapeDtypeStruct(shape, dtype)


def _dot(a, b):
    return jnp.dot(a, b, preferred_element_type=F32)


def _dot_t(a, b):
    return lax.dot_general(a, b, (((1,), (1,)), ((), ())), preferred_element_type=F32)


def _leading(c):
    p = c * 65537.0
    return p - (p - c)


def _two(c):
    high = _leading(c)
    return jnp.concatenate([high, c - high], axis=0).astype(BF16)


def _mul(c, w):
    rows = c.shape[0]
    both = _dot(_two(c), w)
    return both[:rows] + both[rows:]


def _mul_t(c, w):
    rows = c.shape[0]
    both = _dot_t(_two(c), w)
    return both[:rows] + both[rows:]


def _swap_halves(x):
    half = x.shape[-1] // 2
    return jnp.concatenate([x[:, half:], x[:, :half]], axis=1)


def _pair(a, b):
    return jnp.concatenate([a, b], axis=1)


def _request_kernel(anchor_ref, leaves_ref, table_ref, plan_ref):
    me = lax.axis_index("leaf")
    pairs = anchor_ref.shape[1]
    anchor = anchor_ref[...]
    source = leaves_ref[0:1, :]
    my_z = me // GROUP
    my_k = me % GROUP
    core = anchor & 1
    dz = ((anchor >> GROUP_BITS) - my_z) & 7
    near_side = (dz & 3) == 0
    server = jnp.where(near_side, core, jnp.where(dz > 4, 0, 1))
    step = jnp.where(dz > 4, 8 - dz, dz)
    base = jnp.where(
        dz == 0,
        0,
        jnp.where(dz == 4, 224, 32 + (step - 1) * 64 + (core ^ server) * 32),
    )
    tile = base + (source >> 1)
    group = (((anchor & 6) | server) ^ my_k)
    sub8 = lax.broadcasted_iota(jnp.int32, (8, pairs), 0)
    picked = (sub8 == group).astype(F32)
    row = lax.broadcasted_iota(jnp.int32, (pairs, pairs), 0)
    col = lax.broadcasted_iota(jnp.int32, (pairs, pairs), 1)
    upto = (row <= col).astype(F32).astype(BF16)
    count = _dot(picked.astype(BF16), upto)
    slot = (jnp.sum(picked * count, axis=0, keepdims=True) - 1.0).astype(jnp.int32)
    flip = (source ^ slot) & 1
    sub128 = lax.broadcasted_iota(jnp.int32, (128, pairs), 0)
    placed = (sub128 == slot).astype(F32).astype(BF16)
    table = _dot_t((picked * tile.astype(F32)).astype(BF16), placed)
    flips = _dot_t((picked * flip.astype(F32)).astype(BF16), placed)
    table_ref[...] = (table + 256.0 * flips).astype(jnp.int32)
    halves = jnp.floor((count[:, pairs - 1 : pairs] + 1.0) * 0.5)
    before = jnp.sum(jnp.where(sub8 < group, halves, 0.0), axis=0, keepdims=True)
    position = before.astype(jnp.int32) + (slot >> 1)
    even = (slot & 1) == 0
    number = lax.broadcasted_iota(jnp.int32, (1, pairs), 1)
    wanted = leaves_ref[1:2, :]

    def only(which, value):
        return jnp.where(which, value, 0).astype(F32)

    odd = jnp.logical_not(even)
    facts = jnp.concatenate(
        [
            only(even, group * 32 + (slot >> 1)),
            only(even, number),
            only(odd, number),
            only(even, wanted),
            only(odd, wanted),
            only(even, jnp.ones_like(slot)),
            only(odd, jnp.ones_like(slot)),
            jnp.zeros((1, pairs), F32),
        ],
        axis=0,
    )
    listed = (row == position).astype(F32).astype(BF16)
    plan = _dot_t(facts.astype(BF16), listed)
    plan_ref[0:3, :] = plan[0:3].astype(jnp.int32)
    plan_ref[3:4, :] = (plan[3:4] + 64.0 * (1.0 - plan[5:6])).astype(jnp.int32)
    plan_ref[4:5, :] = (plan[4:5] + 64.0 * (1.0 - plan[6:7])).astype(jnp.int32)
    total = jnp.sum(halves, axis=0, keepdims=True)
    plan_ref[5:8, :] = jnp.broadcast_to(total, (3, pairs)).astype(jnp.int32)


LEAF_TILES = 32
OWN_TILES = LEAF_TILES + 1


def _split_points(coords):
    c = coords - 0.5
    high = _leading(c)
    return high, _leading(c - high)


def _prepare_kernel(
    vec_ref, basis_ref, move_ref, own_ref, coeff_ref, levels_ref
):
    leaves = basis_ref.shape[0]
    lane = lax.broadcasted_iota(jnp.int32, (16, 128), 1)

    current = []
    for i in range(leaves // 2):
        x0 = vec_ref[:, 256 * i : 256 * i + 128]
        x1 = vec_ref[:, 256 * i + 128 : 256 * i + 256]
        w = basis_ref[2 * i : 2 * i + 2].reshape(128, 128)
        r = _dot_t(jnp.concatenate([x0, x1], axis=0), w)
        c = jnp.where(lane < 64, r[:16], r[16:])
        coeff_ref[i] = c
        own_ref[i] = c.astype(BF16)
        current.append(c)

    size, node = leaves // 2, leaves
    while True:
        parents = [
            _mul(current[i], move_ref[node + 2 * i : node + 2 * i + 2].reshape(128, 64))
            for i in range(size)
        ]
        if size == 1:
            root = parents[0]
            break
        size //= 2
        node //= 2
        current = [_pair(parents[2 * i], parents[2 * i + 1]) for i in range(size)]
        for i in range(size):
            levels_ref[size + i] = current[i]
    levels_ref[0] = jnp.zeros((16, 128), F32)
    passed = _pair(_mul(root, move_ref[1]), root).astype(BF16)
    own_ref[LEAF_TILES] = passed


def _edges_kernel(p0, p1, p2, p3, vec_ref, give_ref, edge_ref):
    me = lax.axis_index("leaf")
    mine = lax.axis_index("vec")
    core = me & 1
    leaves = vec_ref.shape[1] // 128

    width = p0.shape[1]
    halo = REACH * 128

    def end(last):
        block, lanes = (3, slice(width - halo, width)) if last else (0, slice(0, halo))
        chosen = p0[:, lanes]
        for turn, ref in ((1, p1), (2, p2), (3, p3)):
            chosen = jnp.where(((mine + turn) & 3) == block, ref[:, lanes], chosen)
        return chosen

    def place(ref, at, coords, first):
        high, mid = _split_points(coords)
        both = jnp.concatenate([high, mid, jnp.zeros((10, halo), F32)], axis=0).astype(BF16)
        for j in range(REACH):
            lanes = pl.ds(pl.multiple_of((first + j) * 128, 128), 128)
            ref[at + j] = vec_ref[:, lanes]
            ref[at + REACH + j] = both[:, 128 * j : 128 * j + 128]

    low, high = end(False), end(True)
    place(give_ref, 0, jnp.where(core == 0, high, low), jnp.where(core == 0, leaves - REACH, 0))
    place(edge_ref, 0, jnp.where(core == 0, low, high), jnp.where(core == 0, 0, leaves - REACH))


def _inner_kernel(coeff_ref, levels_ref, move_ref, pair_ref, out_ref, couple_ref):
    lane = lax.broadcasted_iota(jnp.int32, (16, 128), 1)
    couple_ref[...] = pair_ref[1]
    parents = None
    size = 1
    while True:
        children = []
        for i in range(size):
            node = 2 * size + 2 * i
            tile = coeff_ref[i] if size == LEAF_TILES else levels_ref[size + i]
            other = _swap_halves(tile)
            both = _mul(
                jnp.concatenate(
                    [jnp.where(lane < 64, other, 0.0), jnp.where(lane < 64, 0.0, other)], axis=0
                ),
                pair_ref[node : node + 2].reshape(128, 64),
            )
            child = _pair(both[:16], both[16:])
            if parents is not None:
                child = child + _mul_t(parents[i], move_ref[node : node + 2].reshape(128, 64))
            children.append(child)
        if size == LEAF_TILES:
            break
        parents = []
        for c in children:
            parents += [c[:, :64], c[:, 64:]]
        size *= 2
    for i in range(LEAF_TILES):
        out_ref[i] = children[i]


def _from_root(root_local, move_ref):
    parents = [root_local]
    size = 1
    while True:
        children = [
            _mul_t(parents[i], move_ref[2 * size + 2 * i : 2 * size + 2 * i + 2].reshape(128, 64))
            for i in range(size)
        ]
        if size == LEAF_TILES:
            return children
        parents = []
        for c in children:
            parents += [c[:, :64], c[:, 64:]]
        size *= 2


def _root_local(mate_passed, got, move_ref, couple_ref, upper_t_ref, upper_c_ref, c5, c4, c3, c2, c1):
    me = lax.axis_index("leaf")
    my_k = me % GROUP
    my_z = me // GROUP
    my_x = my_k >> 1

    def chip(x, c, tile):
        return got[(2 * x + c) ^ my_k, tile].astype(F32)

    for x in range(4):
        c5[my_z * 4 + x] = chip(x, 0, 0)[:, 0:64]
        for c, sign in ((0, -1), (1, 1)):
            one, two = chip(x, c, 0), chip(x, c, 1)
            steps = [one[:, 64:128], two[:, 0:64], two[:, 64:128]]
            for i in range(3):
                c5[((my_z + sign * (i + 1)) & 7) * 4 + x] = steps[i]
        c5[((my_z + 4) & 7) * 4 + x] = chip(x, 0, 2)[:, 0:64] + chip(x, 1, 2)[:, 0:64]
    count = 32
    for below, above in ((c5, c4), (c4, c3), (c3, c2), (c2, c1)):
        for i in range(count // 2):
            node = count + 2 * i
            above[i] = _mul(
                _pair(below[2 * i], below[2 * i + 1]), upper_t_ref[node : node + 2].reshape(128, 64)
            )
        count //= 2
    place = my_z * 4 + my_x
    sibs = [
        mate_passed[:, 64:128].astype(F32),
        c5[place ^ 1],
        c4[(place >> 1) ^ 1],
        c3[(place >> 2) ^ 1],
        c2[(place >> 3) ^ 1],
        c1[(place >> 4) ^ 1],
    ]
    node = 64 + me
    coupled = [_mul(sibs[bit], upper_c_ref[node >> bit] if bit else couple_ref[...]) for bit in range(6)]
    local = coupled[5]
    for bit in range(4, -1, -1):
        local = _mul_t(local, upper_t_ref[node >> bit] if bit else move_ref[1]) + coupled[bit]
    return local


def _tree_kernel(
    pair_in, g0, g1, g2, g3, g4, g5, g6, g7, inner_ref, move_ref, couple_ref, upper_t_ref, upper_c_ref,
    out_ref, got, c5, c4, c3, c2, c1,
):
    for k, ref in enumerate((g0, g1, g2, g3, g4, g5, g6, g7)):
        got[k] = ref[LEAF_TILES : LEAF_TILES + 3]
    root_local = _root_local(
        pair_in[OWN_TILES + LEAF_TILES], got, move_ref, couple_ref, upper_t_ref, upper_c_ref, c5, c4, c3, c2, c1
    )
    down = _from_root(root_local, move_ref)
    for i in range(LEAF_TILES):
        out_ref[i] = inner_ref[i] + down[i]


def _both_ways(scratch, blocks):
    at = 0
    for ref, first in blocks:
        x = ref[first : first + LEAF_TILES]
        scratch[at : at + LEAF_TILES] = x
        y = _swap_halves(x.reshape(LEAF_TILES * 16, 128)).reshape(LEAF_TILES, 16, 128)
        scratch[256 + at : 256 + at + LEAF_TILES] = y
        at += LEAF_TILES


def _gather_kernel(t0, t1, t2, t3, pair, r1, r2, r3, r4, *rest):
    tables = (t0, t1, t2, t3)
    outs, scratch = rest[:GROUP], rest[GROUP]
    blocks = [(pair, 0)]
    for ref in (r1, r2, r3):
        blocks += [(ref, 0), (ref, OWN_TILES)]
    _both_ways(scratch, blocks + [(r4, 0)])
    lane = lax.broadcasted_iota(jnp.int32, (16, 128), 1)

    def chip(ref):
        return (ref[LEAF_TILES].astype(F32) + ref[OWN_TILES + LEAF_TILES].astype(F32))[:, :64]

    passed = [
        _pair(chip(pair), chip(r1)).astype(BF16),
        _pair(chip(r2), chip(r3)).astype(BF16),
        r4[LEAF_TILES],
    ]
    for k in range(GROUP):
        for s in range(LEAF_TILES):
            a = scratch[tables[k // 2][k % 2, k, 2 * s]]
            b = scratch[tables[k // 2][k % 2, k, 2 * s + 1]]
            outs[k][s] = jnp.where(lane < 64, a, b)
        for i in range(3):
            outs[k][LEAF_TILES + i] = passed[i]


def _features(high, mid):
    width = high.shape[1]
    rounded = high + mid
    square = rounded * rounded
    norm = square[0:1] + square[1:2] + square[2:3]

    def thirds(n):
        n1 = _leading(n)
        n2 = _leading(n - n1)
        return [n1, n2, n - n1 - n2]

    one = jnp.ones((3, width), F32)
    zero = jnp.zeros((2, width), F32)
    pad = jnp.zeros((8, width), F32)
    own = [high, mid, zero]
    source = jnp.concatenate(own + own + thirds(norm + DELTA_SQ) + [one, zero, pad], axis=0)
    target = jnp.concatenate(
        [-2.0 * high, -2.0 * high, zero, -2.0 * mid, -2.0 * mid, zero, one] + thirds(norm) + [zero, pad],
        axis=0,
    )
    return source, target


TOGETHER = 8


def _near_kernel(
    part, parts, cols_ref, p0, p1, p2, p3, vec_ref, mate_ref, edge_ref, out_ref, rows, values, targets, kernel
):
    me = lax.axis_index("leaf")
    mine = lax.axis_index("vec")
    core = me & 1
    leaves = cols_ref.shape[1]
    near, count = cols_ref.shape[0], leaves // parts
    begin = part * count
    per = p0.shape[1] // 128

    beyond = jnp.where(core == 0, REACH + leaves, 0)
    for ref, first, at in ((mate_ref, 0, beyond), (edge_ref, 0, REACH + leaves - beyond)):
        for j in range(REACH):
            both = ref[first + REACH + j].astype(F32)
            features = _features(both[0:3], both[3:6])[0]
            rows[at + j] = jnp.transpose(features).astype(BF16)
            values[at + j] = ref[first + j]
    for turn, ref in enumerate((p0, p1, p2, p3)):
        block = (mine + turn) & 3
        features, target = _features(*_split_points(ref[...]))
        for j in range(per):
            at = block * per + j
            rows[REACH + at] = jnp.transpose(features[:, 128 * j : 128 * j + 128]).astype(BF16)
            targets[at] = target[:, 128 * j : 128 * j + 128].astype(BF16)
    for i in range(leaves):
        values[REACH + i] = vec_ref[:, 128 * i : 128 * i + 128]

    shift = REACH - me * leaves

    def group(step, carry):
        for g in range(TOGETHER):
            t = begin + step * TOGETHER + g
            target = targets[t]
            for k in range(near):
                dist = _dot(rows[cols_ref[k, t] + shift], target)
                kernel[g, 128 * k : 128 * k + 128] = lax.rsqrt(dist).astype(BF16)
        for g in range(TOGETHER):
            t = begin + step * TOGETHER + g
            value = jnp.concatenate([values[cols_ref[k, t] + shift] for k in range(near)], axis=1)
            lanes = pl.ds(pl.multiple_of((step * TOGETHER + g) * 128, 128), 128)
            out_ref[:, lanes] = _dot(value, kernel[g]) * KERNEL_SCALE
        return carry

    lax.fori_loop(0, count // TOGETHER, group, 0)


BATCH = 8


def _final_kernel(plan_ref, r0, r1, r2, r3, r4, r5, r6, r7, block_ref, local_ref, basis_ref, *rest):
    nears, (out_ref, got, far) = rest[:NEAR_PARTS], rest[NEAR_PARTS:]
    for k, ref in enumerate((r0, r1, r2, r3, r4, r5, r6, r7)):
        got[32 * k : 32 * k + 32] = ref[0:LEAF_TILES]
    far[...] = jnp.zeros_like(far)
    lane = lax.broadcasted_iota(jnp.int32, (16, 128), 1)

    def split(x):
        zero = jnp.zeros_like(x)
        return jnp.concatenate([jnp.where(lane < 64, x, zero), jnp.where(lane < 64, zero, x)], axis=0)

    def add(step, carry):
        sums = []
        for i in range(BATCH):
            j = step * BATCH + i
            w = jnp.concatenate([block_ref[plan_ref[1, j]], block_ref[plan_ref[2, j]]], axis=0)
            sums.append(_dot(split(got[plan_ref[0, j]]), w))
        for i in range(BATCH):
            j = step * BATCH + i
            far[plan_ref[3, j]] += sums[i][:16]
            far[plan_ref[4, j]] += sums[i][16:]
        return carry

    lax.fori_loop(0, (plan_ref[5, 0] + BATCH - 1) // BATCH, add, 0)
    for i in range(basis_ref.shape[0] // 2):
        total = (local_ref[i] + _pair(far[2 * i], far[2 * i + 1])).astype(BF16)
        r = _dot(split(total), basis_ref[2 * i : 2 * i + 2].reshape(128, 128))
        at = 256 * i
        near_ref, off = nears[at // nears[0].shape[1]], at % nears[0].shape[1]
        out_ref[:, at : at + 128] = near_ref[:, off : off + 128] + r[:16]
        out_ref[:, at + 128 : at + 256] = near_ref[:, off + 128 : off + 256] + r[16:]


def per_device(
    vectors,
    points,
    leaf_basis,
    local_transfer,
    local_coupling,
    upper_transfer,
    upper_coupling,
    far_anchor,
    far_leaves,
    far_block,
    near_cols,
):
    n_leaf = lax.axis_size("leaf")
    n_vec = lax.axis_size("vec")
    everyone = range(n_leaf)

    def permute(x, to):
        return lax.ppermute(x, "leaf", [(i, to(i)) for i in everyone])

    def after(x, *done):
        return lax.optimization_barrier((x, done))[0]

    def tiles(count, dtype=BF16):
        return _shape((count, 16, 128), dtype)

    width = vectors.shape[1]
    leaves = leaf_basis.shape[0]

    own, coeff, levels = _call(
        _prepare_kernel,
        [tiles(OWN_TILES), tiles(LEAF_TILES, F32), tiles(LEAF_TILES, F32)],
        3,
        flops=1 << 26,
        name="prepare",
    )(vectors, leaf_basis, local_transfer)
    mate = permute(own, lambda i: i ^ 1)

    table, plan = _call(
        _request_kernel,
        [_shape((8, 128), jnp.int32), _shape((8, far_anchor.shape[0]), jnp.int32)],
        2,
        flops=1 << 22,
        name="request",
    )(*after((far_anchor.reshape(1, -1), far_leaves.T), own))
    chip = jnp.stack([table, permute(table, lambda i: i ^ 1)])
    tables = [chip] + [permute(chip, lambda i, x=x: i ^ 2 * x) for x in (1, 2, 3)]

    def onward(i):
        z, rest = i // GROUP, i % GROUP
        return (z + 1 if i % 2 == 0 else z - 1) % (n_leaf // GROUP) * GROUP + rest

    pair = jnp.concatenate([own, mate], axis=0)
    ring1 = permute(pair, onward)

    def by_rows(x, done):
        return with_layout_constraint(after(x, done), Layout(major_to_minor=(0, 1, 2)))

    far_block = by_rows(far_block, pair)
    ring2 = permute(after(ring1, far_block), onward)
    local_coupling = by_rows(local_coupling, ring1)
    ring3 = permute(after(ring2, local_coupling, tables), onward)

    points = after(points, ring2)
    turns = [points] + [
        lax.ppermute(points, "vec", [((i + s) % n_vec, i) for i in range(n_vec)]) for s in range(1, n_vec)
    ]
    ring4 = permute(after(ring3, turns)[:OWN_TILES], onward)
    give, edge = _call(
        _edges_kernel, [tiles(2 * REACH), tiles(2 * REACH)], 5, flops=1 << 22, name="edges"
    )(*turns, vectors)
    sides = (
        permute(give, lambda i: i ^ 1),
        lax.ppermute(
            edge,
            "leaf",
            [(i, i - 1 + 2 * (i % 2)) for i in range(n_leaf) if 0 <= i - 1 + 2 * (i % 2) < n_leaf],
        ),
    )
    inner, couple = _call(
        _inner_kernel,
        [tiles(LEAF_TILES, F32), _shape((64, 64), BF16)],
        4,
        flops=1 << 28,
        name="inner",
    )(*after((coeff, levels), ring3), local_transfer, local_coupling)


    rows = _call(
        _gather_kernel,
        [tiles(LEAF_TILES + 3)] * GROUP,
        9,
        smem=(0, 1, 2, 3),
        scratch=[pltpu.VMEM((512, 16, 128), BF16)],
        flops=1 << 22,
        name="gather",
    )(*after(tables, inner, sides), pair, ring1, ring2, ring3, ring4)

    got = [rows[0]] + [permute(rows[k], lambda i, k=k: i ^ k) for k in range(1, GROUP)]

    blocks = leaves + 2 * REACH

    def near_part(part, done):
        args = after((near_cols.T, *turns, vectors, *sides), done)
        return _call(
            functools.partial(_near_kernel, part, NEAR_PARTS),
            _shape((vectors.shape[0], width // NEAR_PARTS), F32),
            8,
            smem=(0,),
            scratch=[
                pltpu.VMEM((blocks, 128, 32), BF16),
                pltpu.VMEM((blocks, 16, 128), BF16),
                pltpu.VMEM((leaves, 32, 128), BF16),
                pltpu.VMEM((TOGETHER, 1024, 128), BF16),
            ],
            flops=1 << 31,
            name="near%d" % part,
            mib=12,
        )(*args)

    near = [near_part(part, rows[0]) for part in range(NEAR_PARTS)]

    local = _call(
        _tree_kernel,
        tiles(LEAF_TILES, F32),
        14,
        scratch=[pltpu.VMEM((GROUP, 3, 16, 128), BF16)] + [pltpu.VMEM((n, 16, 64), F32) for n in (32, 16, 8, 4, 2)],
        flops=1 << 26,
        name="tree",
    )(pair, *got, inner, local_transfer, couple, upper_transfer, upper_coupling)
    return _call(
        _final_kernel,
        _shape(vectors.shape, F32),
        12 + NEAR_PARTS,
        smem=(0,),
        scratch=[pltpu.VMEM((256, 16, 128), BF16), pltpu.VMEM((65, 16, 64), F32)],
        flops=1 << 27,
        name="final",
        mib=16,
    )(plan, *got, far_block, local, leaf_basis, *near)


def solution(mesh):
    return jax.shard_map(
        per_device,
        mesh=mesh,
        in_specs=(
            P("vec", "leaf"),
            P(None, ("leaf", "vec")),
            P("leaf", None, None),
            P("leaf", None, None),
            P("leaf", None, None),
            P(),
            P(),
            P("leaf", None),
            P("leaf", None),
            P("leaf", None, None),
            P("leaf", None),
        ),
        out_specs=P("vec", "leaf"),
        check_vma=False,
    )
```

```python
import functools

import jax
import jax.numpy as jnp
from jax import lax
from jax.experimental import pallas as pl
from jax.experimental.layout import Layout, with_layout_constraint
from jax.experimental.pallas import tpu as pltpu
from jax.sharding import PartitionSpec as P

F32 = jnp.float32
BF16 = jnp.bfloat16
REACH = 8
KERNEL_SCALE = 1.0 / 64.0
DELTA_SQ = 0.0025

GROUP = 8
GROUP_BITS = 3

NEAR_PARTS = 1


def _spec(space=pltpu.VMEM):
    return pl.BlockSpec(memory_space=space)


def _call(body, outs, n_in, smem=(), scratch=(), flops=0, name=None, mib=8, hbm=()):
    return pl.pallas_call(
        body,
        out_shape=outs,
        in_specs=[
            _spec(pltpu.SMEM if i in smem else pltpu.HBM if i in hbm else pltpu.VMEM) for i in range(n_in)
        ],
        out_specs=jax.tree.map(lambda _: _spec(), outs),
        scratch_shapes=list(scratch),
        compiler_params=pltpu.CompilerParams(vmem_limit_bytes=mib * 1024 * 1024),
        cost_estimate=pl.CostEstimate(flops=flops, bytes_accessed=1 << 20, transcendentals=0),
        name=name,
    )


def _shape(shape, dtype):
    return jax.ShapeDtypeStruct(shape, dtype)


def _dot(a, b):
    return jnp.dot(a, b, preferred_element_type=F32)


def _dot_t(a, b):
    return lax.dot_general(a, b, (((1,), (1,)), ((), ())), preferred_element_type=F32)


def _leading(c):
    p = c * 65537.0
    return p - (p - c)


def _two(c):
    high = _leading(c)
    return jnp.concatenate([high, c - high], axis=0).astype(BF16)


def _mul(c, w):
    rows = c.shape[0]
    both = _dot(_two(c), w)
    return both[:rows] + both[rows:]


def _mul_t(c, w):
    rows = c.shape[0]
    both = _dot_t(_two(c), w)
    return both[:rows] + both[rows:]


def _swap_halves(x):
    half = x.shape[-1] // 2
    return jnp.concatenate([x[:, half:], x[:, :half]], axis=1)


def _pair(a, b):
    return jnp.concatenate([a, b], axis=1)


def _request_kernel(anchor_ref, leaves_ref, table_ref, plan_ref):
    me = lax.axis_index("leaf")
    pairs = anchor_ref.shape[1]
    anchor = anchor_ref[...]
    source = leaves_ref[0:1, :]
    my_z = me // GROUP
    my_k = me % GROUP
    core = anchor & 1
    dz = ((anchor >> GROUP_BITS) - my_z) & 7
    near_side = (dz & 3) == 0
    server = jnp.where(near_side, core, jnp.where(dz > 4, 0, 1))
    step = jnp.where(dz > 4, 8 - dz, dz)
    base = jnp.where(
        dz == 0,
        0,
        jnp.where(dz == 4, 224, 32 + (step - 1) * 64 + (core ^ server) * 32),
    )
    tile = base + (source >> 1)
    group = (((anchor & 6) | server) ^ my_k)
    sub8 = lax.broadcasted_iota(jnp.int32, (8, pairs), 0)
    picked = (sub8 == group).astype(F32)
    row = lax.broadcasted_iota(jnp.int32, (pairs, pairs), 0)
    col = lax.broadcasted_iota(jnp.int32, (pairs, pairs), 1)
    upto = (row <= col).astype(F32).astype(BF16)
    count = _dot(picked.astype(BF16), upto)
    slot = (jnp.sum(picked * count, axis=0, keepdims=True) - 1.0).astype(jnp.int32)
    flip = (source ^ slot) & 1
    sub128 = lax.broadcasted_iota(jnp.int32, (128, pairs), 0)
    placed = (sub128 == slot).astype(F32).astype(BF16)
    table = _dot_t((picked * tile.astype(F32)).astype(BF16), placed)
    flips = _dot_t((picked * flip.astype(F32)).astype(BF16), placed)
    table_ref[...] = (table + 256.0 * flips).astype(jnp.int32)
    halves = jnp.floor((count[:, pairs - 1 : pairs] + 1.0) * 0.5)
    before = jnp.sum(jnp.where(sub8 < group, halves, 0.0), axis=0, keepdims=True)
    position = before.astype(jnp.int32) + (slot >> 1)
    even = (slot & 1) == 0
    number = lax.broadcasted_iota(jnp.int32, (1, pairs), 1)
    wanted = leaves_ref[1:2, :]

    def only(which, value):
        return jnp.where(which, value, 0).astype(F32)

    odd = jnp.logical_not(even)
    facts = jnp.concatenate(
        [
            only(even, group * 32 + (slot >> 1)),
            only(even, number),
            only(odd, number),
            only(even, wanted),
            only(odd, wanted),
            only(even, jnp.ones_like(slot)),
            only(odd, jnp.ones_like(slot)),
            jnp.zeros((1, pairs), F32),
        ],
        axis=0,
    )
    listed = (row == position).astype(F32).astype(BF16)
    plan = _dot_t(facts.astype(BF16), listed)
    plan_ref[0:3, :] = plan[0:3].astype(jnp.int32)
    plan_ref[3:4, :] = (plan[3:4] + 64.0 * (1.0 - plan[5:6])).astype(jnp.int32)
    plan_ref[4:5, :] = (plan[4:5] + 64.0 * (1.0 - plan[6:7])).astype(jnp.int32)
    total = jnp.sum(halves, axis=0, keepdims=True)
    plan_ref[5:8, :] = jnp.broadcast_to(total, (3, pairs)).astype(jnp.int32)


LEAF_TILES = 32
OWN_TILES = LEAF_TILES + 1


def _split_points(coords):
    c = coords - 0.5
    high = _leading(c)
    return high, _leading(c - high)


def _prepare_kernel(
    vec_ref, basis_ref, move_ref, own_ref, nodes_ref
):
    leaves = basis_ref.shape[0]
    lane = lax.broadcasted_iota(jnp.int32, (16, 128), 1)

    current = []
    for i in range(leaves // 2):
        x0 = vec_ref[:, 256 * i : 256 * i + 128]
        x1 = vec_ref[:, 256 * i + 128 : 256 * i + 256]
        w = basis_ref[2 * i : 2 * i + 2].reshape(128, 128)
        r = _dot_t(jnp.concatenate([x0, x1], axis=0), w)
        c = jnp.where(lane < 64, r[:16], r[16:])
        nodes_ref[LEAF_TILES + i] = c
        own_ref[i] = c.astype(BF16)
        current.append(c)

    size, node = leaves // 2, leaves
    while True:
        parents = [
            _mul(current[i], move_ref[node + 2 * i : node + 2 * i + 2].reshape(128, 64))
            for i in range(size)
        ]
        if size == 1:
            root = parents[0]
            break
        size //= 2
        node //= 2
        current = [_pair(parents[2 * i], parents[2 * i + 1]) for i in range(size)]
        for i in range(size):
            nodes_ref[size + i] = current[i]
    nodes_ref[0] = jnp.zeros((16, 128), F32)
    passed = _pair(_mul(root, move_ref[1]), root).astype(BF16)
    own_ref[LEAF_TILES] = passed


def _edges_kernel(p0, p1, p2, p3, vec_ref, give_ref, edge_ref):
    me = lax.axis_index("leaf")
    mine = lax.axis_index("vec")
    core = me & 1
    leaves = vec_ref.shape[1] // 128

    width = p0.shape[1]
    halo = REACH * 128

    def end(last):
        block, lanes = (3, slice(width - halo, width)) if last else (0, slice(0, halo))
        chosen = p0[:, lanes]
        for turn, ref in ((1, p1), (2, p2), (3, p3)):
            chosen = jnp.where(((mine + turn) & 3) == block, ref[:, lanes], chosen)
        return chosen

    def place(ref, at, coords, first):
        high, mid = _split_points(coords)
        both = jnp.concatenate([high, mid, jnp.zeros((10, halo), F32)], axis=0).astype(BF16)
        for j in range(REACH):
            lanes = pl.ds(pl.multiple_of((first + j) * 128, 128), 128)
            ref[at + j] = vec_ref[:, lanes]
            ref[at + REACH + j] = both[:, 128 * j : 128 * j + 128]

    low, high = end(False), end(True)
    place(give_ref, 0, jnp.where(core == 0, high, low), jnp.where(core == 0, leaves - REACH, 0))
    place(edge_ref, 0, jnp.where(core == 0, low, high), jnp.where(core == 0, 0, leaves - REACH))


def _inner_kernel(nodes_ref, move_ref, pair_ref, out_ref, couple_ref):
    lane = lax.broadcasted_iota(jnp.int32, (16, 128), 1)
    couple_ref[...] = pair_ref[1]
    parents = None
    size = 1
    while True:
        children = []
        for i in range(size):
            node = 2 * size + 2 * i
            other = _swap_halves(nodes_ref[size + i])
            both = _mul(
                jnp.concatenate(
                    [jnp.where(lane < 64, other, 0.0), jnp.where(lane < 64, 0.0, other)], axis=0
                ),
                pair_ref[node : node + 2].reshape(128, 64),
            )
            child = _pair(both[:16], both[16:])
            if parents is not None:
                child = child + _mul_t(parents[i], move_ref[node : node + 2].reshape(128, 64))
            children.append(child)
        if size == LEAF_TILES:
            break
        parents = []
        for c in children:
            parents += [c[:, :64], c[:, 64:]]
        size *= 2
    for i in range(LEAF_TILES):
        out_ref[i] = children[i]


def _from_root(root_local, move_ref):
    parents = [root_local]
    size = 1
    while True:
        children = [
            _mul_t(parents[i], move_ref[2 * size + 2 * i : 2 * size + 2 * i + 2].reshape(128, 64))
            for i in range(size)
        ]
        if size == LEAF_TILES:
            return children
        parents = []
        for c in children:
            parents += [c[:, :64], c[:, 64:]]
        size *= 2


def _root_local(mate_passed, got, move_ref, couple_ref, upper_t_ref, upper_c_ref, c5, c4, c3, c2, c1):
    me = lax.axis_index("leaf")
    my_k = me % GROUP
    my_z = me // GROUP
    my_x = my_k >> 1

    def chip(x, c, tile):
        return got[(2 * x + c) ^ my_k, tile].astype(F32)

    for x in range(4):
        c5[my_z * 4 + x] = chip(x, 0, 0)[:, 0:64]
        for c, sign in ((0, -1), (1, 1)):
            one, two = chip(x, c, 0), chip(x, c, 1)
            steps = [one[:, 64:128], two[:, 0:64], two[:, 64:128]]
            for i in range(3):
                c5[((my_z + sign * (i + 1)) & 7) * 4 + x] = steps[i]
        c5[((my_z + 4) & 7) * 4 + x] = chip(x, 0, 2)[:, 0:64] + chip(x, 1, 2)[:, 0:64]
    count = 32
    for below, above in ((c5, c4), (c4, c3), (c3, c2), (c2, c1)):
        for i in range(count // 2):
            node = count + 2 * i
            above[i] = _mul(
                _pair(below[2 * i], below[2 * i + 1]), upper_t_ref[node : node + 2].reshape(128, 64)
            )
        count //= 2
    place = my_z * 4 + my_x
    sibs = [
        mate_passed[:, 64:128].astype(F32),
        c5[place ^ 1],
        c4[(place >> 1) ^ 1],
        c3[(place >> 2) ^ 1],
        c2[(place >> 3) ^ 1],
        c1[(place >> 4) ^ 1],
    ]
    node = 64 + me
    coupled = [_mul(sibs[bit], upper_c_ref[node >> bit] if bit else couple_ref[...]) for bit in range(6)]
    local = coupled[5]
    for bit in range(4, -1, -1):
        local = _mul_t(local, upper_t_ref[node >> bit] if bit else move_ref[1]) + coupled[bit]
    return local


def _tree_kernel(
    pair_in, g0, g1, g2, g3, g4, g5, g6, g7, inner_ref, move_ref, couple_ref, upper_t_ref, upper_c_ref,
    out_ref, got, c5, c4, c3, c2, c1,
):
    for k, ref in enumerate((g0, g1, g2, g3, g4, g5, g6, g7)):
        got[k] = ref[LEAF_TILES : LEAF_TILES + 3]
    root_local = _root_local(
        pair_in[OWN_TILES + LEAF_TILES], got, move_ref, couple_ref, upper_t_ref, upper_c_ref, c5, c4, c3, c2, c1
    )
    down = _from_root(root_local, move_ref)
    for i in range(LEAF_TILES):
        out_ref[i] = inner_ref[i] + down[i]


def _both_ways(scratch, blocks):
    at = 0
    for ref, first in blocks:
        x = ref[first : first + LEAF_TILES]
        scratch[at : at + LEAF_TILES] = x
        y = _swap_halves(x.reshape(LEAF_TILES * 16, 128)).reshape(LEAF_TILES, 16, 128)
        scratch[256 + at : 256 + at + LEAF_TILES] = y
        at += LEAF_TILES


def _gather_kernel(t0, t1, t2, t3, pair, r1, r2, r3, r4, *rest):
    tables = (t0, t1, t2, t3)
    outs, scratch = rest[:GROUP], rest[GROUP]
    blocks = [(pair, 0)]
    for ref in (r1, r2, r3):
        blocks += [(ref, 0), (ref, OWN_TILES)]
    _both_ways(scratch, blocks + [(r4, 0)])
    lane = lax.broadcasted_iota(jnp.int32, (16, 128), 1)

    def chip(ref):
        return (ref[LEAF_TILES].astype(F32) + ref[OWN_TILES + LEAF_TILES].astype(F32))[:, :64]

    passed = [
        _pair(chip(pair), chip(r1)).astype(BF16),
        _pair(chip(r2), chip(r3)).astype(BF16),
        r4[LEAF_TILES],
    ]
    for k in range(GROUP):
        for s in range(LEAF_TILES):
            a = scratch[tables[k // 2][k % 2, k, 2 * s]]
            b = scratch[tables[k // 2][k % 2, k, 2 * s + 1]]
            outs[k][s] = jnp.where(lane < 64, a, b)
        for i in range(3):
            outs[k][LEAF_TILES + i] = passed[i]


def _features(high, mid):
    width = high.shape[1]
    rounded = high + mid
    square = rounded * rounded
    norm = square[0:1] + square[1:2] + square[2:3]

    def thirds(n):
        n1 = _leading(n)
        n2 = _leading(n - n1)
        return [n1, n2, n - n1 - n2]

    one = jnp.ones((3, width), F32)
    zero = jnp.zeros((2, width), F32)
    pad = jnp.zeros((8, width), F32)
    own = [high, mid, zero]
    source = jnp.concatenate(own + own + thirds(norm + DELTA_SQ) + [one, zero, pad], axis=0)
    target = jnp.concatenate(
        [-2.0 * high, -2.0 * high, zero, -2.0 * mid, -2.0 * mid, zero, one] + thirds(norm) + [zero, pad],
        axis=0,
    )
    return source, target


TOGETHER = 16


def _near_kernel(
    part, parts, cols_ref, p0, p1, p2, p3, vec_ref, mate_ref, edge_ref, out_ref, rows, values, targets, kernel
):
    me = lax.axis_index("leaf")
    mine = lax.axis_index("vec")
    core = me & 1
    leaves = cols_ref.shape[1]
    near, count = cols_ref.shape[0], leaves // parts
    begin = part * count
    per = p0.shape[1] // 128

    beyond = jnp.where(core == 0, REACH + leaves, 0)
    for ref, first, at in ((mate_ref, 0, beyond), (edge_ref, 0, REACH + leaves - beyond)):
        for j in range(REACH):
            both = ref[first + REACH + j].astype(F32)
            features = _features(both[0:3], both[3:6])[0]
            rows[at + j] = jnp.transpose(features).astype(BF16)
            values[at + j] = ref[first + j]
    for turn, ref in enumerate((p0, p1, p2, p3)):
        block = (mine + turn) & 3
        features, target = _features(*_split_points(ref[...]))
        for j in range(per):
            at = block * per + j
            rows[REACH + at] = jnp.transpose(features[:, 128 * j : 128 * j + 128]).astype(BF16)
            targets[at] = target[:, 128 * j : 128 * j + 128].astype(BF16)
    for i in range(leaves):
        values[REACH + i] = vec_ref[:, 128 * i : 128 * i + 128]

    shift = REACH - me * leaves

    def group(step, carry):
        for g in range(TOGETHER):
            t = begin + step * TOGETHER + g
            target = targets[t]
            for k in range(near):
                dist = _dot(rows[cols_ref[k, t] + shift], target)
                kernel[g, 128 * k : 128 * k + 128] = lax.rsqrt(dist).astype(BF16)
        for g in range(TOGETHER):
            t = begin + step * TOGETHER + g
            value = jnp.concatenate([values[cols_ref[k, t] + shift] for k in range(near)], axis=1)
            lanes = pl.ds(pl.multiple_of((step * TOGETHER + g) * 128, 128), 128)
            out_ref[:, lanes] = _dot(value, kernel[g]) * KERNEL_SCALE
        return carry

    lax.fori_loop(0, count // TOGETHER, group, 0)


BATCH = 16


def _final_kernel(plan_ref, r0, r1, r2, r3, r4, r5, r6, r7, block_ref, local_ref, basis_ref, *rest):
    nears, (out_ref, got, far) = rest[:NEAR_PARTS], rest[NEAR_PARTS:]
    for k, ref in enumerate((r0, r1, r2, r3, r4, r5, r6, r7)):
        got[32 * k : 32 * k + 32] = ref[0:LEAF_TILES]
    far[...] = jnp.zeros_like(far)
    lane = lax.broadcasted_iota(jnp.int32, (16, 128), 1)

    def split(x):
        zero = jnp.zeros_like(x)
        return jnp.concatenate([jnp.where(lane < 64, x, zero), jnp.where(lane < 64, zero, x)], axis=0)

    def add(step, carry):
        sums = []
        for i in range(BATCH):
            j = step * BATCH + i
            w = jnp.concatenate([block_ref[plan_ref[1, j]], block_ref[plan_ref[2, j]]], axis=0)
            sums.append(_dot(split(got[plan_ref[0, j]]), w))
        for i in range(BATCH):
            j = step * BATCH + i
            far[plan_ref[3, j]] += sums[i][:16]
            far[plan_ref[4, j]] += sums[i][16:]
        return carry

    lax.fori_loop(0, (plan_ref[5, 0] + BATCH - 1) // BATCH, add, 0)
    for i in range(basis_ref.shape[0] // 2):
        total = (local_ref[i] + _pair(far[2 * i], far[2 * i + 1])).astype(BF16)
        r = _dot(split(total), basis_ref[2 * i : 2 * i + 2].reshape(128, 128))
        at = 256 * i
        near_ref, off = nears[at // nears[0].shape[1]], at % nears[0].shape[1]
        out_ref[:, at : at + 128] = near_ref[:, off : off + 128] + r[:16]
        out_ref[:, at + 128 : at + 256] = near_ref[:, off + 128 : off + 256] + r[16:]


def per_device(
    vectors,
    points,
    leaf_basis,
    local_transfer,
    local_coupling,
    upper_transfer,
    upper_coupling,
    far_anchor,
    far_leaves,
    far_block,
    near_cols,
):
    n_leaf = lax.axis_size("leaf")
    n_vec = lax.axis_size("vec")
    everyone = range(n_leaf)

    def permute(x, to):
        return lax.ppermute(x, "leaf", [(i, to(i)) for i in everyone])

    def after(x, *done):
        return lax.optimization_barrier((x, done))[0]

    def tiles(count, dtype=BF16):
        return _shape((count, 16, 128), dtype)

    width = vectors.shape[1]
    leaves = leaf_basis.shape[0]

    own, nodes = _call(
        _prepare_kernel,
        [tiles(OWN_TILES), tiles(2 * LEAF_TILES, F32)],
        3,
        flops=1 << 26,
        name="prepare",
    )(vectors, leaf_basis, local_transfer)
    mate = permute(own, lambda i: i ^ 1)

    table, plan = _call(
        _request_kernel,
        [_shape((8, 128), jnp.int32), _shape((8, far_anchor.shape[0]), jnp.int32)],
        2,
        flops=1 << 22,
        name="request",
    )(*after((far_anchor.reshape(1, -1), far_leaves.T), own))
    chip = jnp.stack([table, permute(table, lambda i: i ^ 1)])
    tables = [chip] + [permute(chip, lambda i, x=x: i ^ 2 * x) for x in (1, 2, 3)]

    def onward(i):
        z, rest = i // GROUP, i % GROUP
        return (z + 1 if i % 2 == 0 else z - 1) % (n_leaf // GROUP) * GROUP + rest

    pair = jnp.concatenate([own, mate], axis=0)
    ring1 = permute(pair, onward)

    def by_rows(x, done):
        return with_layout_constraint(after(x, done), Layout(major_to_minor=(0, 1, 2)))

    far_block = by_rows(far_block, pair)
    ring2 = permute(after(ring1, far_block), onward)
    local_coupling = by_rows(local_coupling, ring1)
    ring3 = permute(after(ring2, local_coupling, tables), onward)

    points = after(points, ring2)
    turns = [points] + [
        lax.ppermute(points, "vec", [((i + s) % n_vec, i) for i in range(n_vec)]) for s in range(1, n_vec)
    ]
    ring4 = permute(after(ring3, turns)[:OWN_TILES], onward)
    give, edge = _call(
        _edges_kernel, [tiles(2 * REACH), tiles(2 * REACH)], 5, flops=1 << 22, name="edges"
    )(*turns, vectors)
    sides = (
        permute(give, lambda i: i ^ 1),
        lax.ppermute(
            edge,
            "leaf",
            [(i, i - 1 + 2 * (i % 2)) for i in range(n_leaf) if 0 <= i - 1 + 2 * (i % 2) < n_leaf],
        ),
    )
    inner, couple = _call(
        _inner_kernel,
        [tiles(LEAF_TILES, F32), _shape((64, 64), BF16)],
        3,
        flops=1 << 28,
        name="inner",
    )(after(nodes, ring3), local_transfer, local_coupling)


    rows = _call(
        _gather_kernel,
        [tiles(LEAF_TILES + 3)] * GROUP,
        9,
        smem=(0, 1, 2, 3),
        scratch=[pltpu.VMEM((512, 16, 128), BF16)],
        flops=1 << 22,
        name="gather",
    )(*after(tables, inner, sides), pair, ring1, ring2, ring3, ring4)

    got = [rows[0]] + [permute(rows[k], lambda i, k=k: i ^ k) for k in range(1, GROUP)]

    blocks = leaves + 2 * REACH

    def near_part(part, done):
        args = after((near_cols.T, *turns, vectors, *sides), done)
        return _call(
            functools.partial(_near_kernel, part, NEAR_PARTS),
            _shape((vectors.shape[0], width // NEAR_PARTS), F32),
            8,
            smem=(0,),
            scratch=[
                pltpu.VMEM((blocks, 128, 32), BF16),
                pltpu.VMEM((blocks, 16, 128), BF16),
                pltpu.VMEM((leaves, 32, 128), BF16),
                pltpu.VMEM((TOGETHER, 1024, 128), BF16),
            ],
            flops=1 << 31,
            name="near%d" % part,
            mib=12,
        )(*args)

    near = [near_part(part, rows[0]) for part in range(NEAR_PARTS)]

    local = _call(
        _tree_kernel,
        tiles(LEAF_TILES, F32),
        14,
        scratch=[pltpu.VMEM((GROUP, 3, 16, 128), BF16)] + [pltpu.VMEM((n, 16, 64), F32) for n in (32, 16, 8, 4, 2)],
        flops=1 << 26,
        name="tree",
    )(pair, *got, inner, local_transfer, couple, upper_transfer, upper_coupling)
    return _call(
        _final_kernel,
        _shape(vectors.shape, F32),
        12 + NEAR_PARTS,
        smem=(0,),
        scratch=[pltpu.VMEM((256, 16, 128), BF16), pltpu.VMEM((65, 16, 64), F32)],
        flops=1 << 27,
        name="final",
        mib=16,
    )(plan, *got, far_block, local, leaf_basis, *near)


def solution(mesh):
    return jax.shard_map(
        per_device,
        mesh=mesh,
        in_specs=(
            P("vec", "leaf"),
            P(None, ("leaf", "vec")),
            P("leaf", None, None),
            P("leaf", None, None),
            P("leaf", None, None),
            P(),
            P(),
            P("leaf", None),
            P("leaf", None),
            P("leaf", None, None),
            P("leaf", None),
        ),
        out_specs=P("vec", "leaf"),
        check_vma=False,
    )
```

```python
import functools

import jax
import jax.numpy as jnp
from jax import lax
from jax.experimental import pallas as pl
from jax.experimental.layout import Layout, with_layout_constraint
from jax.experimental.pallas import tpu as pltpu
from jax.sharding import PartitionSpec as P

F32 = jnp.float32
BF16 = jnp.bfloat16
REACH = 8
KERNEL_SCALE = 1.0 / 64.0
DELTA_SQ = 0.0025

GROUP = 8
GROUP_BITS = 3

NEAR_PARTS = 1


def _spec(space=pltpu.VMEM):
    return pl.BlockSpec(memory_space=space)


def _call(body, outs, n_in, smem=(), scratch=(), flops=0, name=None, mib=8, hbm=()):
    return pl.pallas_call(
        body,
        out_shape=outs,
        in_specs=[
            _spec(pltpu.SMEM if i in smem else pltpu.HBM if i in hbm else pltpu.VMEM) for i in range(n_in)
        ],
        out_specs=jax.tree.map(lambda _: _spec(), outs),
        scratch_shapes=list(scratch),
        compiler_params=pltpu.CompilerParams(vmem_limit_bytes=mib * 1024 * 1024),
        cost_estimate=pl.CostEstimate(flops=flops, bytes_accessed=1 << 20, transcendentals=0),
        name=name,
    )


def _shape(shape, dtype):
    return jax.ShapeDtypeStruct(shape, dtype)


def _dot(a, b):
    return jnp.dot(a, b, preferred_element_type=F32)


def _dot_t(a, b):
    return lax.dot_general(a, b, (((1,), (1,)), ((), ())), preferred_element_type=F32)


def _leading(c):
    p = c * 65537.0
    return p - (p - c)


def _two(c):
    high = _leading(c)
    return jnp.concatenate([high, c - high], axis=0).astype(BF16)


def _mul(c, w):
    rows = c.shape[0]
    both = _dot(_two(c), w)
    return both[:rows] + both[rows:]


def _mul_t(c, w):
    rows = c.shape[0]
    both = _dot_t(_two(c), w)
    return both[:rows] + both[rows:]


def _swap_halves(x):
    half = x.shape[-1] // 2
    return jnp.concatenate([x[:, half:], x[:, :half]], axis=1)


def _pair(a, b):
    return jnp.concatenate([a, b], axis=1)


def _request_kernel(anchor_ref, leaves_ref, table_ref, plan_ref):
    me = lax.axis_index("leaf")
    pairs = anchor_ref.shape[1]
    anchor = anchor_ref[...]
    source = leaves_ref[0:1, :]
    my_z = me // GROUP
    my_k = me % GROUP
    core = anchor & 1
    dz = ((anchor >> GROUP_BITS) - my_z) & 7
    near_side = (dz & 3) == 0
    server = jnp.where(near_side, core, jnp.where(dz > 4, 0, 1))
    step = jnp.where(dz > 4, 8 - dz, dz)
    base = jnp.where(
        dz == 0,
        0,
        jnp.where(dz == 4, 224, 32 + (step - 1) * 64 + (core ^ server) * 32),
    )
    tile = base + (source >> 1)
    group = (((anchor & 6) | server) ^ my_k)
    sub8 = lax.broadcasted_iota(jnp.int32, (8, pairs), 0)
    picked = (sub8 == group).astype(F32)
    row = lax.broadcasted_iota(jnp.int32, (pairs, pairs), 0)
    col = lax.broadcasted_iota(jnp.int32, (pairs, pairs), 1)
    upto = (row <= col).astype(F32).astype(BF16)
    count = _dot(picked.astype(BF16), upto)
    slot = (jnp.sum(picked * count, axis=0, keepdims=True) - 1.0).astype(jnp.int32)
    flip = (source ^ slot) & 1
    sub128 = lax.broadcasted_iota(jnp.int32, (128, pairs), 0)
    placed = (sub128 == slot).astype(F32).astype(BF16)
    table = _dot_t((picked * tile.astype(F32)).astype(BF16), placed)
    flips = _dot_t((picked * flip.astype(F32)).astype(BF16), placed)
    table_ref[...] = (table + 256.0 * flips).astype(jnp.int32)
    halves = jnp.floor((count[:, pairs - 1 : pairs] + 1.0) * 0.5)
    before = jnp.sum(jnp.where(sub8 < group, halves, 0.0), axis=0, keepdims=True)
    position = before.astype(jnp.int32) + (slot >> 1)
    even = (slot & 1) == 0
    number = lax.broadcasted_iota(jnp.int32, (1, pairs), 1)
    wanted = leaves_ref[1:2, :]

    def only(which, value):
        return jnp.where(which, value, 0).astype(F32)

    odd = jnp.logical_not(even)
    facts = jnp.concatenate(
        [
            only(even, group * 32 + (slot >> 1)),
            only(even, number),
            only(odd, number),
            only(even, wanted),
            only(odd, wanted),
            only(even, jnp.ones_like(slot)),
            only(odd, jnp.ones_like(slot)),
            jnp.zeros((1, pairs), F32),
        ],
        axis=0,
    )
    listed = (row == position).astype(F32).astype(BF16)
    plan = _dot_t(facts.astype(BF16), listed)
    plan_ref[0:3, :] = plan[0:3].astype(jnp.int32)
    plan_ref[3:4, :] = (plan[3:4] + 64.0 * (1.0 - plan[5:6])).astype(jnp.int32)
    plan_ref[4:5, :] = (plan[4:5] + 64.0 * (1.0 - plan[6:7])).astype(jnp.int32)
    total = jnp.sum(halves, axis=0, keepdims=True)
    plan_ref[5:8, :] = jnp.broadcast_to(total, (3, pairs)).astype(jnp.int32)


LEAF_TILES = 32
OWN_TILES = LEAF_TILES + 1


def _split_points(coords):
    c = coords - 0.5
    high = _leading(c)
    return high, _leading(c - high)


def _prepare_kernel(
    vec_ref, basis_ref, move_ref, own_ref, nodes_ref
):
    leaves = basis_ref.shape[0]
    lane = lax.broadcasted_iota(jnp.int32, (16, 128), 1)

    current = []
    for i in range(leaves // 2):
        x0 = vec_ref[:, 256 * i : 256 * i + 128]
        x1 = vec_ref[:, 256 * i + 128 : 256 * i + 256]
        w = basis_ref[2 * i : 2 * i + 2].reshape(128, 128)
        r = _dot_t(jnp.concatenate([x0, x1], axis=0), w)
        c = jnp.where(lane < 64, r[:16], r[16:])
        nodes_ref[LEAF_TILES + i] = c
        own_ref[i] = c.astype(BF16)
        current.append(c)

    size, node = leaves // 2, leaves
    while True:
        parents = [
            _mul(current[i], move_ref[node + 2 * i : node + 2 * i + 2].reshape(128, 64))
            for i in range(size)
        ]
        if size == 1:
            root = parents[0]
            break
        size //= 2
        node //= 2
        current = [_pair(parents[2 * i], parents[2 * i + 1]) for i in range(size)]
        for i in range(size):
            nodes_ref[size + i] = current[i]
    nodes_ref[0] = jnp.zeros((16, 128), F32)
    passed = _pair(_mul(root, move_ref[1]), root).astype(BF16)
    own_ref[LEAF_TILES] = passed


def _edges_kernel(p0, p1, p2, p3, vec_ref, give_ref, edge_ref):
    me = lax.axis_index("leaf")
    mine = lax.axis_index("vec")
    core = me & 1
    leaves = vec_ref.shape[1] // 128

    width = p0.shape[1]
    halo = REACH * 128

    def end(last):
        block, lanes = (3, slice(width - halo, width)) if last else (0, slice(0, halo))
        chosen = p0[:, lanes]
        for turn, ref in ((1, p1), (2, p2), (3, p3)):
            chosen = jnp.where(((mine + turn) & 3) == block, ref[:, lanes], chosen)
        return chosen

    def place(ref, at, coords, first):
        high, mid = _split_points(coords)
        both = jnp.concatenate([high, mid, jnp.zeros((10, halo), F32)], axis=0).astype(BF16)
        for j in range(REACH):
            lanes = pl.ds(pl.multiple_of((first + j) * 128, 128), 128)
            ref[at + j] = vec_ref[:, lanes]
            ref[at + REACH + j] = both[:, 128 * j : 128 * j + 128]

    low, high = end(False), end(True)
    place(give_ref, 0, jnp.where(core == 0, high, low), jnp.where(core == 0, leaves - REACH, 0))
    place(edge_ref, 0, jnp.where(core == 0, low, high), jnp.where(core == 0, 0, leaves - REACH))


def _inner_kernel(nodes_ref, move_ref, pair_ref, out_ref, couple_ref):
    lane = lax.broadcasted_iota(jnp.int32, (16, 128), 1)
    couple_ref[...] = pair_ref[1]
    parents = None
    size = 1
    while True:
        children = []
        for i in range(size):
            node = 2 * size + 2 * i
            other = _swap_halves(nodes_ref[size + i])
            both = _mul(
                jnp.concatenate(
                    [jnp.where(lane < 64, other, 0.0), jnp.where(lane < 64, 0.0, other)], axis=0
                ),
                pair_ref[node : node + 2].reshape(128, 64),
            )
            child = _pair(both[:16], both[16:])
            if parents is not None:
                child = child + _mul_t(parents[i], move_ref[node : node + 2].reshape(128, 64))
            children.append(child)
        if size == LEAF_TILES:
            break
        parents = []
        for c in children:
            parents += [c[:, :64], c[:, 64:]]
        size *= 2
    for i in range(LEAF_TILES):
        out_ref[i] = children[i]


def _from_root(root_local, move_ref):
    parents = [root_local]
    size = 1
    while True:
        children = [
            _mul_t(parents[i], move_ref[2 * size + 2 * i : 2 * size + 2 * i + 2].reshape(128, 64))
            for i in range(size)
        ]
        if size == LEAF_TILES:
            return children
        parents = []
        for c in children:
            parents += [c[:, :64], c[:, 64:]]
        size *= 2


def _root_local(mate_passed, got, move_ref, couple_ref, upper_t_ref, upper_c_ref, c5, c4, c3, c2, c1):
    me = lax.axis_index("leaf")
    my_k = me % GROUP
    my_z = me // GROUP
    my_x = my_k >> 1

    def chip(x, c, tile):
        return got[(2 * x + c) ^ my_k, tile].astype(F32)

    for x in range(4):
        c5[my_z * 4 + x] = chip(x, 0, 0)[:, 0:64]
        for c, sign in ((0, -1), (1, 1)):
            one, two = chip(x, c, 0), chip(x, c, 1)
            steps = [one[:, 64:128], two[:, 0:64], two[:, 64:128]]
            for i in range(3):
                c5[((my_z + sign * (i + 1)) & 7) * 4 + x] = steps[i]
        c5[((my_z + 4) & 7) * 4 + x] = chip(x, 0, 2)[:, 0:64] + chip(x, 1, 2)[:, 0:64]
    count = 32
    for below, above in ((c5, c4), (c4, c3), (c3, c2), (c2, c1)):
        for i in range(count // 2):
            node = count + 2 * i
            above[i] = _mul(
                _pair(below[2 * i], below[2 * i + 1]), upper_t_ref[node : node + 2].reshape(128, 64)
            )
        count //= 2
    place = my_z * 4 + my_x
    sibs = [
        mate_passed[:, 64:128].astype(F32),
        c5[place ^ 1],
        c4[(place >> 1) ^ 1],
        c3[(place >> 2) ^ 1],
        c2[(place >> 3) ^ 1],
        c1[(place >> 4) ^ 1],
    ]
    node = 64 + me
    coupled = [_mul(sibs[bit], upper_c_ref[node >> bit] if bit else couple_ref[...]) for bit in range(6)]
    local = coupled[5]
    for bit in range(4, -1, -1):
        local = _mul_t(local, upper_t_ref[node >> bit] if bit else move_ref[1]) + coupled[bit]
    return local


def _tree_kernel(
    pair_in, g0, g1, g2, g3, g4, g5, g6, g7, inner_ref, move_ref, couple_ref, upper_t_ref, upper_c_ref,
    out_ref, got, c5, c4, c3, c2, c1,
):
    for k, ref in enumerate((g0, g1, g2, g3, g4, g5, g6, g7)):
        got[k] = ref[LEAF_TILES : LEAF_TILES + 3]
    root_local = _root_local(
        pair_in[OWN_TILES + LEAF_TILES], got, move_ref, couple_ref, upper_t_ref, upper_c_ref, c5, c4, c3, c2, c1
    )
    down = _from_root(root_local, move_ref)
    for i in range(LEAF_TILES):
        out_ref[i] = inner_ref[i] + down[i]


def _both_ways(scratch, blocks):
    at = 0
    for ref, first in blocks:
        x = ref[first : first + LEAF_TILES]
        scratch[at : at + LEAF_TILES] = x
        y = _swap_halves(x.reshape(LEAF_TILES * 16, 128)).reshape(LEAF_TILES, 16, 128)
        scratch[256 + at : 256 + at + LEAF_TILES] = y
        at += LEAF_TILES


def _gather_kernel(t0, t1, t2, t3, pair, r1, r2, r3, r4, *rest):
    tables = (t0, t1, t2, t3)
    outs, scratch = rest[:GROUP], rest[GROUP]
    blocks = [(pair, 0)]
    for ref in (r1, r2, r3):
        blocks += [(ref, 0), (ref, OWN_TILES)]
    _both_ways(scratch, blocks + [(r4, 0)])
    lane = lax.broadcasted_iota(jnp.int32, (16, 128), 1)

    def chip(ref):
        return (ref[LEAF_TILES].astype(F32) + ref[OWN_TILES + LEAF_TILES].astype(F32))[:, :64]

    passed = [
        _pair(chip(pair), chip(r1)).astype(BF16),
        _pair(chip(r2), chip(r3)).astype(BF16),
        r4[LEAF_TILES],
    ]
    for k in range(GROUP):
        for s in range(LEAF_TILES):
            a = scratch[tables[k // 2][k % 2, k, 2 * s]]
            b = scratch[tables[k // 2][k % 2, k, 2 * s + 1]]
            outs[k][s] = jnp.where(lane < 64, a, b)
        for i in range(3):
            outs[k][LEAF_TILES + i] = passed[i]


def _features(high, mid):
    width = high.shape[1]
    rounded = high + mid
    square = rounded * rounded
    norm = square[0:1] + square[1:2] + square[2:3]

    def thirds(n):
        n1 = _leading(n)
        n2 = _leading(n - n1)
        return [n1, n2, n - n1 - n2]

    one = jnp.ones((3, width), F32)
    zero = jnp.zeros((2, width), F32)
    pad = jnp.zeros((8, width), F32)
    own = [high, mid, zero]
    source = jnp.concatenate(own + own + thirds(norm + DELTA_SQ) + [one, zero, pad], axis=0)
    target = jnp.concatenate(
        [-2.0 * high, -2.0 * high, zero, -2.0 * mid, -2.0 * mid, zero, one] + thirds(norm) + [zero, pad],
        axis=0,
    )
    return source, target


TOGETHER = 16


def _near_kernel(
    part, parts, cols_ref, p0, p1, p2, p3, vec_ref, mate_ref, edge_ref, out_ref, rows, values, targets, kernel
):
    me = lax.axis_index("leaf")
    mine = lax.axis_index("vec")
    core = me & 1
    leaves = cols_ref.shape[1]
    near, count = cols_ref.shape[0], leaves // parts
    begin = part * count
    per = p0.shape[1] // 128

    beyond = jnp.where(core == 0, REACH + leaves, 0)
    for ref, first, at in ((mate_ref, 0, beyond), (edge_ref, 0, REACH + leaves - beyond)):
        for j in range(REACH):
            both = ref[first + REACH + j].astype(F32)
            features = _features(both[0:3], both[3:6])[0]
            rows[at + j] = jnp.transpose(features).astype(BF16)
            values[at + j] = ref[first + j]
    for turn, ref in enumerate((p0, p1, p2, p3)):
        block = (mine + turn) & 3
        features, target = _features(*_split_points(ref[...]))
        for j in range(per):
            at = block * per + j
            rows[REACH + at] = jnp.transpose(features[:, 128 * j : 128 * j + 128]).astype(BF16)
            targets[at] = target[:, 128 * j : 128 * j + 128].astype(BF16)
    for i in range(leaves):
        values[REACH + i] = vec_ref[:, 128 * i : 128 * i + 128]

    shift = REACH - me * leaves

    def group(step, carry):
        for g in range(TOGETHER):
            t = begin + step * TOGETHER + g
            target = targets[t]
            for k in range(near):
                dist = _dot(rows[cols_ref[k, t] + shift], target)
                kernel[g, 128 * k : 128 * k + 128] = lax.rsqrt(dist).astype(BF16)
        for g in range(TOGETHER):
            t = begin + step * TOGETHER + g
            value = jnp.concatenate([values[cols_ref[k, t] + shift] for k in range(near)], axis=1)
            lanes = pl.ds(pl.multiple_of((step * TOGETHER + g) * 128, 128), 128)
            out_ref[:, lanes] = _dot(value, kernel[g]) * KERNEL_SCALE
        return carry

    lax.fori_loop(0, count // TOGETHER, group, 0)


BATCH = 16


def _final_kernel(plan_ref, r0, r1, r2, r3, r4, r5, r6, r7, block_ref, local_ref, basis_ref, *rest):
    nears, (out_ref, got, far) = rest[:NEAR_PARTS], rest[NEAR_PARTS:]
    for k, ref in enumerate((r0, r1, r2, r3, r4, r5, r6, r7)):
        got[32 * k : 32 * k + 32] = ref[0:LEAF_TILES]
    far[...] = jnp.zeros_like(far)
    lane = lax.broadcasted_iota(jnp.int32, (16, 128), 1)

    def split(x):
        zero = jnp.zeros_like(x)
        return jnp.concatenate([jnp.where(lane < 64, x, zero), jnp.where(lane < 64, zero, x)], axis=0)

    def add(step, carry):
        sums = []
        for i in range(BATCH):
            j = step * BATCH + i
            w = jnp.concatenate([block_ref[plan_ref[1, j]], block_ref[plan_ref[2, j]]], axis=0)
            sums.append(_dot(split(got[plan_ref[0, j]]), w))
        for i in range(BATCH):
            j = step * BATCH + i
            far[plan_ref[3, j]] += sums[i][:16]
            far[plan_ref[4, j]] += sums[i][16:]
        return carry

    lax.fori_loop(0, (plan_ref[5, 0] + BATCH - 1) // BATCH, add, 0)
    for i in range(basis_ref.shape[0] // 2):
        total = (local_ref[i] + _pair(far[2 * i], far[2 * i + 1])).astype(BF16)
        r = _dot(split(total), basis_ref[2 * i : 2 * i + 2].reshape(128, 128))
        at = 256 * i
        near_ref, off = nears[at // nears[0].shape[1]], at % nears[0].shape[1]
        out_ref[:, at : at + 128] = near_ref[:, off : off + 128] + r[:16]
        out_ref[:, at + 128 : at + 256] = near_ref[:, off + 128 : off + 256] + r[16:]


def per_device(
    vectors,
    points,
    leaf_basis,
    local_transfer,
    local_coupling,
    upper_transfer,
    upper_coupling,
    far_anchor,
    far_leaves,
    far_block,
    near_cols,
):
    n_leaf = lax.axis_size("leaf")
    n_vec = lax.axis_size("vec")
    everyone = range(n_leaf)

    def permute(x, to):
        return lax.ppermute(x, "leaf", [(i, to(i)) for i in everyone])

    def after(x, *done):
        return lax.optimization_barrier((x, done))[0]

    def tiles(count, dtype=BF16):
        return _shape((count, 16, 128), dtype)

    width = vectors.shape[1]
    leaves = leaf_basis.shape[0]

    own, nodes = _call(
        _prepare_kernel,
        [tiles(OWN_TILES), tiles(2 * LEAF_TILES, F32)],
        3,
        flops=1 << 26,
        name="prepare",
    )(vectors, leaf_basis, local_transfer)
    mate = permute(own, lambda i: i ^ 1)

    table, plan = _call(
        _request_kernel,
        [_shape((8, 128), jnp.int32), _shape((8, far_anchor.shape[0]), jnp.int32)],
        2,
        flops=1 << 22,
        name="request",
    )(*after((far_anchor.reshape(1, -1), far_leaves.T), own))
    chip = jnp.stack([table, permute(table, lambda i: i ^ 1)])
    tables = [chip] + [permute(chip, lambda i, x=x: i ^ 2 * x) for x in (1, 2, 3)]

    def onward(i):
        z, rest = i // GROUP, i % GROUP
        return (z + 1 if i % 2 == 0 else z - 1) % (n_leaf // GROUP) * GROUP + rest

    pair = jnp.concatenate([own, mate], axis=0)
    ring1 = permute(pair, onward)

    def by_rows(x, done):
        return with_layout_constraint(after(x, done), Layout(major_to_minor=(0, 1, 2)))

    far_block = by_rows(far_block, pair)
    ring2 = permute(after(ring1, far_block), onward)
    local_coupling = by_rows(local_coupling, ring1)
    ring3 = permute(after(ring2, local_coupling, tables), onward)

    points = after(points, ring2)
    turns = [points] + [
        lax.ppermute(points, "vec", [((i + s) % n_vec, i) for i in range(n_vec)]) for s in range(1, n_vec)
    ]
    ring4 = permute(ring3[:OWN_TILES], onward)
    give, edge = _call(
        _edges_kernel, [tiles(2 * REACH), tiles(2 * REACH)], 5, flops=1 << 22, name="edges"
    )(*turns, vectors)
    sides = (
        permute(give, lambda i: i ^ 1),
        lax.ppermute(
            edge,
            "leaf",
            [(i, i - 1 + 2 * (i % 2)) for i in range(n_leaf) if 0 <= i - 1 + 2 * (i % 2) < n_leaf],
        ),
    )
    inner, couple = _call(
        _inner_kernel,
        [tiles(LEAF_TILES, F32), _shape((64, 64), BF16)],
        3,
        flops=1 << 28,
        name="inner",
    )(after(nodes, ring2), local_transfer, local_coupling)


    rows = _call(
        _gather_kernel,
        [tiles(LEAF_TILES + 3)] * GROUP,
        9,
        smem=(0, 1, 2, 3),
        scratch=[pltpu.VMEM((512, 16, 128), BF16)],
        flops=1 << 22,
        name="gather",
    )(*after(tables, inner, sides), pair, ring1, ring2, ring3, ring4)

    got = [rows[0]] + [permute(rows[k], lambda i, k=k: i ^ k) for k in range(1, GROUP)]

    blocks = leaves + 2 * REACH

    def near_part(part, done):
        args = after((near_cols.T, *turns, vectors, *sides), done)
        return _call(
            functools.partial(_near_kernel, part, NEAR_PARTS),
            _shape((vectors.shape[0], width // NEAR_PARTS), F32),
            8,
            smem=(0,),
            scratch=[
                pltpu.VMEM((blocks, 128, 32), BF16),
                pltpu.VMEM((blocks, 16, 128), BF16),
                pltpu.VMEM((leaves, 32, 128), BF16),
                pltpu.VMEM((TOGETHER, 1024, 128), BF16),
            ],
            flops=1 << 31,
            name="near%d" % part,
            mib=12,
        )(*args)

    near = [near_part(part, rows[0]) for part in range(NEAR_PARTS)]

    local = _call(
        _tree_kernel,
        tiles(LEAF_TILES, F32),
        14,
        scratch=[pltpu.VMEM((GROUP, 3, 16, 128), BF16)] + [pltpu.VMEM((n, 16, 64), F32) for n in (32, 16, 8, 4, 2)],
        flops=1 << 26,
        name="tree",
    )(pair, *got, inner, local_transfer, couple, upper_transfer, upper_coupling)
    return _call(
        _final_kernel,
        _shape(vectors.shape, F32),
        12 + NEAR_PARTS,
        smem=(0,),
        scratch=[pltpu.VMEM((256, 16, 128), BF16), pltpu.VMEM((65, 16, 64), F32)],
        flops=1 << 27,
        name="final",
        mib=16,
    )(plan, *got, far_block, local, leaf_basis, *near)


def solution(mesh):
    return jax.shard_map(
        per_device,
        mesh=mesh,
        in_specs=(
            P("vec", "leaf"),
            P(None, ("leaf", "vec")),
            P("leaf", None, None),
            P("leaf", None, None),
            P("leaf", None, None),
            P(),
            P(),
            P("leaf", None),
            P("leaf", None),
            P("leaf", None, None),
            P("leaf", None),
        ),
        out_specs=P("vec", "leaf"),
        check_vma=False,
    )
```
